32 devices in a mesh: dp: 8 (over z, x), seq: 4 (over y, core).
Axes of the slice: x: 2, y: 2, z: 4, core: 2. Of those that a mesh axis runs over, the one named last changes fastest.
Arguments:
- tokens: bfloat16 [16, 1024, 1024], P('dp', 'seq'), may hold values from -6 to 6
- cotangent: bfloat16 [16, 1024, 1024], P('dp', 'seq'), may hold values from -6 to 6
- src_len: int32 [16], P('dp'), may hold values from 30 to 400
- tgt_len: int32 [16], P('dp'), may hold values from 1 to 994, as said below
- attn_gain: bfloat16 [1024], replicated, may hold values from 0.5 to 1.5
- attn_shift: bfloat16 [1024], replicated, may hold values from -1.75 to 1.75
- qkv_weight: bfloat16 [1024, 3072], replicated, may hold values from -0.1875 to 0.1875
- qkv_bias: bfloat16 [3072], replicated, may hold values from -1.75 to 1.75
- out_weight: bfloat16 [1024, 1024], replicated, may hold values from -1.5 to 1.5
- out_bias: bfloat16 [1024], replicated, may hold values from -1.75 to 1.75
- mlp_gain: bfloat16 [1024], replicated, may hold values from 0.099609375 to 1.8984375
- mlp_shift: bfloat16 [1024], replicated, may hold values from -1.75 to 1.75
- fc_weight: bfloat16 [1024, 4096], replicated, may hold values from -0.1875 to 0.1875
- fc_bias: bfloat16 [4096], replicated, may hold values from -1.75 to 1.75
- proj_weight: bfloat16 [4096, 1024], replicated, may hold values from -0.125 to 0.125
- proj_bias: bfloat16 [1024], replicated, may hold values from -1.75 to 1.75
- embed_rows: bfloat16 [10, 1024], replicated, may hold values from -6 to 6
- mid_weight: bfloat16 [1024, 512], replicated, may hold values from -0.1875 to 0.1875
- mid_bias: bfloat16 [512], replicated, may hold values from -3 to 3
- kv_weight: bfloat16 [512, 2048], replicated, may hold values from -0.5 to 0.5
- kv_bias: bfloat16 [2048], replicated, may hold values from -3 to 3
Outputs:
- hidden_out: bfloat16 [16, 1024, 1024], P('dp', 'seq')
- grad_tokens: bfloat16 [16, 1024, 1024], P('dp', 'seq')
- grad_embed: float32 [10, 1024], replicated
- grad_midw: float32 [1024, 512], replicated
- grad_midb: float32 [512], replicated
- grad_kvw: float32 [512, 2048], replicated
- grad_kvb: float32 [2048], replicated
The draws below stay inside these ranges and needn't reach their ends.
Inputs may be any that keep to these rules, and one draw needn't show every extreme that they name: src_len + tgt_len <= 1024; in every aligned block of 2 rows one row has src_len + tgt_len = 1024.
All inputs are finite; a program needn't handle non-finite values.
Results may differ from the reference program's by a relative error of at most 0.015.
Values may be sent and summed in bfloat16 or wider, within the bound.
A program may use at most 256 MiB of HBM per device.

```python
from functools import partial
import jax
import jax.numpy as jnp
from jax import lax

D = 1024
HEADS = 16
HD = 64
FF = 4096
P_SIZE = 10
PH = 512
L = 1024
ROWS_DEV = 2
ROWS = 16


def draw_lengths(key):
    pick_key, src_key, total_key = jax.random.split(key, 3)
    src_lo = max(1, 30 * L // 1024)
    src_hi = 400 * L // 1024
    source = jax.random.randint(src_key, (ROWS,), src_lo, src_hi + 1)
    totals_drawn = jax.random.randint(total_key, (ROWS,), source + 1, L + 1)
    chosen = jax.random.randint(pick_key, (ROWS // ROWS_DEV,), 0, ROWS_DEV)
    row_index = jnp.arange(ROWS, dtype=jnp.int32)
    full_rows = row_index % ROWS_DEV == jnp.repeat(chosen, ROWS_DEV)
    totals_drawn = jnp.where(full_rows, L, totals_drawn)
    lowest = chosen[0]
    highest = (chosen[0] + 1) % ROWS_DEV
    source = jnp.where(row_index == lowest, src_lo, source)
    source = jnp.where(row_index == highest, src_hi, source)
    totals_drawn = jnp.where(row_index == highest, src_hi + 1, totals_drawn)
    return (source.astype(jnp.int32), (totals_drawn - source).astype(jnp.int32))


def draw_src_len(key, part):
    drawn = draw_lengths(key)
    return drawn[0]


def draw_tgt_len(key, part):
    drawn = draw_lengths(key)
    return drawn[1]


def block_scale(stream_key, dims, cuts, least, largest):
    level = 1.0
    for axis_at, shards_of in cuts:
        draws = jax.random.uniform(jax.random.fold_in(jax.random.fold_in(stream_key, 6), axis_at), (shards_of,), jnp.float32, least / len(cuts), largest / len(cuts))
        level = level * jnp.repeat(jnp.exp(draws), dims[axis_at] // shards_of).reshape((-1,) + (1,) * (len(dims) - 1 - axis_at))
    return level


def bell_draw(stream_key, dims, deviation, most, cuts=(), kind=jnp.bfloat16):
    values = deviation * jax.random.normal(stream_key, dims, jnp.float32)
    if cuts:
        values = values * block_scale(stream_key, dims, cuts, -0.22, 0.18)
    return jnp.clip(values, -most, most).astype(kind)


def setup_inputs(seed: int = 0) -> dict:
    streams_of = jax.random.split(jax.random.key(seed), 22)
    return {
        "tokens": bell_draw(streams_of[0], (ROWS, L, D), 1.0, 6.0, ((0, 8), (1, 4))),
        "cotangent": bell_draw(streams_of[1], (ROWS, L, D), 1.0, 6.0, ((0, 8), (1, 4))),
        "src_len": draw_src_len(jax.random.fold_in(streams_of[21], 71), 0),
        "tgt_len": draw_tgt_len(jax.random.fold_in(streams_of[21], 71), 0),
        "attn_gain": jnp.clip(1.0 + 0.1 * jax.random.normal(streams_of[4], (D,), jnp.float32), 0.5, 1.5).astype(jnp.bfloat16),
        "attn_shift": bell_draw(streams_of[5], (D,), 0.3, 1.75),
        "qkv_weight": bell_draw(streams_of[6], (D, 3 * D), D ** -0.5, 0.1875),
        "qkv_bias": bell_draw(streams_of[7], (3 * D,), 0.3, 1.75),
        "out_weight": bell_draw(streams_of[8], (D, D), (D // 64) ** -0.5, 1.5),
        "out_bias": bell_draw(streams_of[9], (D,), 0.3, 1.75),
        "mlp_gain": jnp.clip(1.0 + 0.18 * jax.random.normal(streams_of[10], (D,), jnp.float32), 0.099609375, 1.8984375).astype(jnp.bfloat16),
        "mlp_shift": bell_draw(streams_of[11], (D,), 0.3, 1.75),
        "fc_weight": bell_draw(streams_of[12], (D, FF), D ** -0.5, 0.1875),
        "fc_bias": bell_draw(streams_of[13], (FF,), 0.3, 1.75),
        "proj_weight": bell_draw(streams_of[14], (FF, D), (FF // 2) ** -0.5, 0.125),
        "proj_bias": bell_draw(streams_of[15], (D,), 0.3, 1.75),
        "embed_rows": bell_draw(streams_of[16], (P_SIZE, D), 1.0, 6.0),
        "mid_weight": bell_draw(streams_of[17], (D, PH), D ** -0.5, 0.1875),
        "mid_bias": bell_draw(streams_of[18], (PH,), 0.5, 3.0),
        "kv_weight": bell_draw(streams_of[19], (PH, 2 * D), (PH // 4) ** -0.5, 0.5),
        "kv_bias": bell_draw(streams_of[20], (2 * D,), 0.5, 3.0),
    }


@jax.custom_vjp
def low(v):
    return lax.optimization_barrier(v.astype(jnp.bfloat16)).astype(jnp.float32)

@jax.custom_vjp
def low_back(v):
    return v

def low_keep(v):
    return (low(v), None)

def low_pass(kept, grad):
    return (grad,)

def back_keep(v):
    return (v, None)

def back_low(kept, grad):
    return (low(grad),)
low.defvjp(low_keep, low_pass)
low_back.defvjp(back_keep, back_low)
EPS = 1e-05
NEG = -1e+30
HIGH = lax.Precision.HIGHEST

def layer_norm(values_in, gain_vec, shift_vec):
    mean_row = lax.optimization_barrier(jnp.mean(values_in, axis=-1, keepdims=True))
    centered = values_in - mean_row
    var_row = lax.optimization_barrier(jnp.mean(centered * centered, axis=-1, keepdims=True))
    return centered * lax.rsqrt(var_row + EPS) * gain_vec + shift_vec

def attend_sequence(pieces, prefix_keys, prefix_vals):
    queries, keys_seq, vals_seq, total_len = pieces
    scaled = queries.reshape(L, HEADS, HD) * HD ** (-0.5)
    keys_cat = jnp.concatenate([prefix_keys, keys_seq]).reshape(P_SIZE + L, HEADS, HD)
    vals_cat = jnp.concatenate([prefix_vals, vals_seq]).reshape(P_SIZE + L, HEADS, HD)
    scores = low_back(jnp.einsum('qhe,khe->hqk', scaled, keys_cat, precision=HIGH))
    positions = jnp.arange(L, dtype=jnp.int32)
    key_pos = jnp.concatenate([jnp.full((P_SIZE,), -1, jnp.int32), positions])
    allowed = (key_pos[None, :] <= positions[:, None]) & (key_pos[None, :] < total_len)
    scores = jnp.where(allowed[None], scores, NEG)
    maxima = lax.optimization_barrier(jnp.max(scores, axis=-1, keepdims=True))
    exp_terms = jnp.exp(scores - maxima)
    probs_row = low(exp_terms / lax.optimization_barrier(jnp.sum(exp_terms, axis=-1, keepdims=True)))
    return jnp.einsum('hqk,khe->qhe', probs_row, vals_cat, precision=HIGH).reshape(L, D)

def rows_forward(pieces, frozen, prefix_keys, prefix_vals):
    rows_in, lengths = pieces
    attn_gain, attn_shift, qkv_weight, qkv_bias, out_weight, out_bias, mlp_gain, mlp_shift, fc_weight, fc_bias, proj_weight, proj_bias = frozen
    normed = low(layer_norm(rows_in, attn_gain, attn_shift))
    mixed_qkv = low(low_back(jnp.einsum('rld,de->rle', normed, qkv_weight, precision=HIGH) + qkv_bias))
    queries = mixed_qkv[..., :D]
    keys_rows = mixed_qkv[..., D:2 * D]
    vals_rows = mixed_qkv[..., 2 * D:]
    attend = jax.checkpoint(partial(attend_sequence, prefix_keys=prefix_keys, prefix_vals=prefix_vals))
    attended = lax.map(attend, (queries, keys_rows, vals_rows, lengths))
    attended = low(low_back(attended))
    branch = low_back(jnp.einsum('rld,de->rle', attended, out_weight, precision=HIGH) + out_bias)
    middle = rows_in + branch
    normed_two = low(layer_norm(middle, mlp_gain, mlp_shift))
    upward = low_back(jnp.einsum('rld,df->rlf', normed_two, fc_weight, precision=HIGH) + fc_bias)
    active = low(jax.nn.gelu(upward, approximate=True))
    return middle + jnp.einsum('rlf,fd->rld', active, proj_weight, precision=HIGH) + proj_bias

def layer_forward(tokens_f, embed_f, midw_f, midb_f, kvw_f, kvb_f, frozen, totals):
    hidden = jnp.tanh(jnp.dot(embed_f, midw_f, precision=HIGH) + midb_f)
    prefix_kv = jnp.dot(hidden, kvw_f, precision=HIGH) + kvb_f
    prefix_keys = low(prefix_kv[:, :D])
    prefix_vals = low(prefix_kv[:, D:])
    grouped = tokens_f.reshape(ROWS // ROWS_DEV, ROWS_DEV, L, D)
    lengths = totals.reshape(ROWS // ROWS_DEV, ROWS_DEV)
    stepper = jax.checkpoint(partial(rows_forward, frozen=frozen, prefix_keys=prefix_keys, prefix_vals=prefix_vals))
    result = lax.map(stepper, (grouped, lengths))
    return result.reshape(ROWS, L, D)

def reference(tokens, cotangent, src_len, tgt_len, attn_gain, attn_shift, qkv_weight, qkv_bias, out_weight, out_bias, mlp_gain, mlp_shift, fc_weight, fc_bias, proj_weight, proj_bias, embed_rows, mid_weight, mid_bias, kv_weight, kv_bias):
    frozen = tuple((array_in.astype(jnp.float32) for array_in in (attn_gain, attn_shift, qkv_weight, qkv_bias, out_weight, out_bias, mlp_gain, mlp_shift, fc_weight, fc_bias, proj_weight, proj_bias)))
    totals = src_len + tgt_len

    def run_layer(tokens_f, embed_f, midw_f, midb_f, kvw_f, kvb_f):
        return layer_forward(tokens_f, embed_f, midw_f, midb_f, kvw_f, kvb_f, frozen, totals)
    result, pull_back = jax.vjp(run_layer, tokens.astype(jnp.float32), embed_rows.astype(jnp.float32), mid_weight.astype(jnp.float32), mid_bias.astype(jnp.float32), kv_weight.astype(jnp.float32), kv_bias.astype(jnp.float32))
    positions = jnp.arange(L, dtype=jnp.int32)
    target = (positions[None, :] >= src_len[:, None]) & (positions[None, :] < totals[:, None])
    cot_f = cotangent.astype(jnp.float32)
    grad_seed = cot_f * target[:, :, None].astype(cot_f.dtype)
    grad_tok, grad_embed, grad_midw, grad_midb, grad_kvw, grad_kvb = pull_back(grad_seed)
    return (result.astype(jnp.bfloat16), grad_tok.astype(jnp.bfloat16), grad_embed, grad_midw, grad_midb, grad_kvw, grad_kvb)
```

```python
import jax
import jax.numpy as jnp
from jax import lax
from jax.experimental import pallas as pl
from jax.experimental.pallas import tpu as pltpu
from jax.sharding import PartitionSpec as P

D = 1024
HD = 64
FF = 4096
PRE = 10
PP = 16
SEG = 256
OWN = 512
NH = 8
NB = 4
EPS = 1e-05
NEG = -1e30
HIGH = lax.Precision.HIGHEST
MESH = pl.DeviceIdType.MESH
f32 = jnp.float32
bf16 = jnp.bfloat16


def mm(a, b, ca=1, cb=0):
    return lax.dot_general(a, b, (((ca,), (cb,)), ((), ())), preferred_element_type=f32)


def centre(v):
    mean = jnp.mean(v, axis=-1, keepdims=True)
    cen = v - mean
    var = jnp.mean(cen * cen, axis=-1, keepdims=True)
    return cen, lax.rsqrt(var + EPS)


def norm_back(v, incoming):
    cen, r = centre(v)
    xhat = cen * r
    m1 = jnp.mean(incoming, axis=-1, keepdims=True)
    m2 = jnp.mean(incoming * xhat, axis=-1, keepdims=True)
    return r * (incoming - m1 - xhat * m2)


def aligned(i, n):
    return pl.multiple_of(i, n)


def split3(v):
    hi = v.astype(bf16)
    rest = v - hi.astype(f32)
    mid = rest.astype(bf16)
    lo = (rest - mid.astype(f32)).astype(bf16)
    return hi, mid, lo


def kernel(
    tok_h, cot_h, src, tgt,
    ag1, ash1, qb1, ob1, mg1, msh1, fb1, pb1, mb1, kvb1,
    wqkv_h, wout_h, wfc_h, wproj_h, emb, midw_h, kvw_h,
    hid_h, gtok_h, gpre,
    wqkv, wout, wfc, wproj,
    tok2, cot2, xn, qm, kx, kT, vx, vT, es, ep, dsp, ot, oTo, oTf,
    mid, yacc, dxacc, dqT, kb, dbias,
    pkT, pvbd, pvT, linv, deltap,
    ag, ash, qb, ob, mg, msh, fb, pb, kvb,
    wsem, lsem, far_s, far_r, xn_s, xn_r, o_s, o_r, d_s, d_r, g_s, g_r, out_s, out_r, loc_out,
):
    s = lax.axis_index("seq")
    y = lax.div(s, 2)
    c = lax.rem(s, 2)
    sib = 2 * y + (1 - c)
    far = 2 * (1 - y) + c
    bl = 2 * y + c
    br = 2 * (1 - y) + c
    cw = aligned(c * OWN, OWN)
    ow = aligned((1 - c) * OWN, OWN)

    def load(i, src_ref, dst_ref):
        cp = pltpu.make_async_copy(src_ref, dst_ref, wsem.at[i])
        cp.start()
        return cp

    ld_tok = load(0, tok_h.at[y], tok2.at[pl.ds(0, SEG)])
    ld_mid0 = load(1, midw_h.at[pl.ds(0, 512)], vT.at[:, pl.ds(0, 512)])
    ld_mid1 = load(2, midw_h.at[pl.ds(512, 512)], vT.at[:, pl.ds(512, 512)])
    ld_kvk = load(3, kvw_h.at[:, pl.ds(cw, OWN)], kT.at[:, pl.ds(0, OWN)])
    ld_kvv = load(4, kvw_h.at[:, pl.ds(aligned(D + c * OWN, OWN), OWN)], kT.at[:, pl.ds(OWN, OWN)])
    ld_qkv = load(5, wqkv_h, wqkv)
    ld_cot = load(6, cot_h.at[y], cot2.at[pl.ds(0, SEG)])
    ld_out = load(7, wout_h, wout)
    ld_fc = load(8, wfc_h, wfc)
    ld_proj = load(9, wproj_h, wproj)

    barrier = pltpu.get_barrier_semaphore()
    for peer in (sib, far):
        pl.semaphore_signal(barrier, inc=1, device_id={"seq": peer}, device_id_type=MESH)
    pl.semaphore_wait(barrier, 2)

    def remote(src_ref, dst_ref, ss, rs, peer):
        return pltpu.make_async_remote_copy(
            src_ref=src_ref, dst_ref=dst_ref, send_sem=ss, recv_sem=rs,
            device_id={"seq": peer}, device_id_type=MESH,
        )

    CH = 64
    NCH = SEG // CH
    tok_cp = [
        remote(
            tok_h.at[1 - y, pl.ds(j * CH, CH)], tok2.at[pl.ds(SEG + j * CH, CH)],
            far_s.at[j], far_r.at[j], far,
        )
        for j in range(NCH)
    ]
    for cp in tok_cp:
        cp.start()
    cot_cp = remote(cot_h.at[1 - y], cot2.at[pl.ds(SEG, SEG)], far_s.at[NCH], far_r.at[NCH], far)

    for dst, vec in ((ag, ag1), (ash, ash1), (qb, qb1), (ob, ob1), (mg, mg1), (msh, msh1), (fb, fb1), (pb, pb1), (kvb, kvb1)):
        n = vec.shape[0]
        for i in range(0, n, 1024):
            dst[:, i : i + 1024] = vec[pl.ds(i, 1024)].astype(f32).reshape(1, 1024)
    total = src[y] + tgt[y]
    start = src[y]
    rowp = lax.broadcasted_iota(jnp.int32, (PP, 128), 0)
    kb[0:PP, :] = jnp.where(rowp < PRE, 0.0, NEG)
    for b in range(NB):
        pos = lax.broadcasted_iota(jnp.int32, (SEG, 128), 0) + b * SEG
        kb[PP + b * SEG : PP + (b + 1) * SEG, :] = jnp.where(pos < total, 0.0, NEG)

    def norm_rows(row0, n, dst0):
        cen, r = centre(tok2[row0 : row0 + n, :].astype(f32))
        xn[pl.ds(aligned(dst0, n), n), :] = (cen * r * ag[...] + ash[...]).astype(bf16)

    ld_tok.wait()
    norm_rows(0, SEG, bl * SEG)
    xl = xn.at[pl.ds(aligned(bl * SEG, SEG), SEG)]
    xl_cp = remote(xl, xl, xn_s.at[NCH], xn_r.at[NCH], sib)
    xl_cp.start()

    ld_mid0.wait()
    ld_mid1.wait()
    embp = jnp.concatenate([emb[...], jnp.zeros((PP - PRE, D), bf16)], axis=0)
    pre = mm(embp[:, 0:512], vT[:, 0:512]) + mm(embp[:, 512:1024], vT[:, 512:1024])
    pre = pre + mb1[...].astype(f32).reshape(1, 512)
    hidden = jnp.tanh(pre)
    ld_kvk.wait()
    ld_kvv.wait()
    h3 = jnp.concatenate(split3(hidden), axis=0)
    pk3 = mm(h3, kT[:, 0:OWN])
    pv3 = mm(h3, kT[:, OWN : 2 * OWN])
    pk = pk3[0:PP] + pk3[PP : 2 * PP] + pk3[2 * PP :] + kvb[:, pl.ds(cw, OWN)]
    pv = pv3[0:PP] + pv3[PP : 2 * PP] + pv3[2 * PP :] + kvb[:, pl.ds(aligned(D + c * OWN, OWN), OWN)]
    for hp in range(4):
        kx[hp, 0:PP, :] = pk[:, hp * 128 : (hp + 1) * 128].astype(bf16)
    hr = lax.broadcasted_iota(jnp.int32, (NH * PP, OWN), 0) // PP
    hc = lax.broadcasted_iota(jnp.int32, (NH * PP, OWN), 1) // HD
    pk8 = jnp.where(hr == hc, jnp.concatenate([pk] * NH, axis=0), 0.0)
    pv8 = jnp.where(hr == hc, jnp.concatenate([pv] * NH, axis=0), 0.0)
    pvbd[...] = pv8.astype(bf16)
    pkT[...] = pk8.T.astype(bf16)
    pvT[...] = pv8.T.astype(bf16)

    lane = lax.broadcasted_iota(jnp.int32, (1, 128), 1)
    lo_half = jnp.where(lane < HD, 1.0, 0.0).astype(bf16)
    hi_half = jnp.where(lane < HD, 0.0, 1.0).astype(bf16)

    def spread(dst, rows, val):
        for hp in range(4):
            pair = val[:, hp * 128 : (hp + 1) * 128]
            dst[rows, 2 * hp * 128 : (2 * hp + 1) * 128] = pair * lo_half
            dst[rows, (2 * hp + 1) * 128 : (2 * hp + 2) * 128] = pair * hi_half

    def project(b):
        rows = pl.ds(aligned(b * SEG, SEG), SEG)
        krows = pl.ds(aligned(PP + b * SEG, PP), SEG)
        x = xn[rows, :]
        q = (mm(x, wqkv[:, pl.ds(cw, OWN)]) + qb[:, pl.ds(cw, OWN)]).astype(bf16) * jnp.asarray(HD ** (-0.5), bf16)
        spread(qm, rows, q)
        kw = pl.ds(aligned(D + c * OWN, OWN), OWN)
        k = (mm(x, wqkv[:, kw]) + qb[:, kw]).astype(bf16)
        kT[:, rows] = k.T
        vw = pl.ds(aligned(2 * D + c * OWN, OWN), OWN)
        v = (mm(x, wqkv[:, vw]) + qb[:, vw]).astype(bf16)
        vT[:, rows] = v.T
        for hp in range(4):
            kx[hp, krows, :] = k[:, hp * 128 : (hp + 1) * 128]
            vx[hp, rows, :] = v[:, hp * 128 : (hp + 1) * 128]

    ld_qkv.wait()
    project(bl)
    xl_cp.wait()
    project(lax.bitwise_xor(bl, 1))

    fw = []
    for j in range(NCH):
        tok_cp[j].wait_recv()
        norm_rows(SEG + j * CH, CH, br * SEG + j * CH)
        xr = xn.at[pl.ds(aligned(br * SEG + j * CH, CH), CH)]
        cp = remote(xr, xr, xn_s.at[j], xn_r.at[j], sib)
        cp.start()
        fw.append(cp)
    for cp in tok_cp:
        cp.wait_send()
    cot_cp.start()
    project(br)
    for cp in fw:
        cp.wait()
    project(lax.bitwise_xor(br, 1))

    def slot_of(b):
        return lax.bitwise_xor(b // 2 if isinstance(b, int) else lax.div(b, 2), y)

    def rep(vals, n):
        return jnp.concatenate([jnp.broadcast_to(vals[h : h + 1], (n, vals.shape[1])) for h in range(NH)], axis=0)

    def twice(v):
        return jnp.concatenate([v, v], axis=1)

    tri = lax.broadcasted_iota(jnp.int32, (SEG, SEG), 0) <= lax.broadcasted_iota(jnp.int32, (SEG, SEG), 1)

    def o_copy(b):
        return remote(
            oTo.at[b], oTf.at[slot_of(b), pl.ds(cw, OWN)], o_s.at[slot_of(b)], o_r.at[slot_of(b)], sib
        )

    for b in (3, 2, 1, 0):
        cols = slice(b * SEG, (b + 1) * SEG)
        low = PP + b * SEG
        off = SEG * (b * (b + 1) // 2)
        dbias[...] = jnp.where(tri, twice(kb[low : low + SEG, :]), NEG)

        def heads(hp, carry, b=b, cols=cols, low=low, off=off):
            for u in range(2):
                h = 2 * hp + u
                qh = qm[cols, pl.ds(aligned(h * 128, 128), 128)]
                s0 = mm(kx[hp, 0:low, :], qh, 1, 1) + twice(kb[0:low, :])
                s1 = mm(kx[hp, low : low + SEG, :], qh, 1, 1) + dbias[...]
                m = jnp.maximum(jnp.max(s0, axis=0, keepdims=True), jnp.max(s1, axis=0, keepdims=True))
                e0 = jnp.exp(s0 - m)
                e1 = jnp.exp(s1 - m)
                den = jnp.sum(e0, axis=0, keepdims=True) + jnp.sum(e1, axis=0, keepdims=True)
                linv[pl.ds(h, 1), cols] = 1.0 / den
                p0 = e0.astype(bf16)
                p1 = e1.astype(bf16)
                ep[pl.ds(aligned(h * PP, PP), PP), cols] = p0[0:PP]
                hrows = pl.ds(aligned(h * HD, HD), HD)
                if b:
                    es[h, off : off + b * SEG, :] = p0[PP:]
                es[h, off + b * SEG : off + (b + 1) * SEG, :] = p1
                ot[hrows, :] = mm(vT[hrows, 0 : (b + 1) * SEG], es[h, off : off + (b + 1) * SEG, :])
            return carry

        lax.fori_loop(0, 4, heads, 0)
        o = (ot[...] + mm(pvT[...], ep[:, cols])) * rep(linv[:, cols], HD)
        oTo[b] = o.astype(bf16)

        @pl.when(c == b % 2)
        def _(b=b):
            oTf[slot_of(b), pl.ds(cw, OWN), :] = oTo[b]

        @pl.when(c != b % 2)
        def _(b=b):
            o_copy(b).start()

    def half_get(ref, sl):
        return jnp.concatenate([ref[sl * SEG : (sl + 1) * SEG, :], ref[OWN + sl * SEG : OWN + (sl + 1) * SEG, :]], axis=1)

    def half_put(ref, sl, val):
        ref[sl * SEG : (sl + 1) * SEG, :] = val[:, 0:OWN]
        ref[OWN + sl * SEG : OWN + (sl + 1) * SEG, :] = val[:, OWN:]

    ld_out.wait()
    ld_cot.wait()
    cot_cp.wait_recv()
    for sl in (0, 1):
        pltpu.make_async_copy(oTf.at[sl, pl.ds(ow, OWN)], oTf.at[sl, pl.ds(ow, OWN)], o_r.at[sl]).wait()
        blk = bl if sl == 0 else br
        m = mm(oTf[sl], wout[...], 0, 0) + ob[...] + tok2[sl * SEG : (sl + 1) * SEG, :].astype(f32)
        half_put(mid, sl, m)
        cen, r = centre(m)
        xn[sl * SEG : (sl + 1) * SEG, :] = (cen * r * mg[...] + msh[...]).astype(bf16)
        pos = lax.broadcasted_iota(jnp.int32, (SEG, 1), 0) + blk * SEG
        seen = jnp.where((pos >= start) & (pos < total), 1.0, 0.0)
        cot2[sl * SEG : (sl + 1) * SEG, :] = (cot2[sl * SEG : (sl + 1) * SEG, :].astype(f32) * seen).astype(bf16)
    for sl in (0, 1):
        pltpu.make_async_copy(oTo.at[sl], oTo.at[sl], o_s.at[sl]).wait()

    ld_fc.wait()
    ld_proj.wait()
    yacc[...] = jnp.zeros_like(yacc)
    dxacc[...] = jnp.zeros_like(dxacc)
    FC = 512

    def feed(i, carry):
        fs = pl.ds(aligned(i * FC, FC), FC)
        u = mm(xn[0:OWN, :], wfc[:, fs]) + fb[:, fs]
        da = mm(cot2[...], wproj[fs, :], 1, 1)
        u2 = u * u
        th = jnp.tanh(u * (0.7978845608028654 + 0.035677408136300125 * u2))
        hh = 0.5 * th + 0.5
        act = u * hh
        slope = hh + act * (1.0 - hh) * (1.5957691216057308 + 0.21406444881780075 * u2)
        ab = act.astype(bf16)
        db = (slope * da).astype(bf16)
        for n in range(2):
            rows = slice(n * OWN, (n + 1) * OWN)
            yacc[rows, :] += mm(ab, wproj[fs, rows])
            dxacc[rows, :] += mm(db, wfc[rows, fs], 1, 1)
        return carry

    lax.fori_loop(0, FF // FC, feed, 0)

    for sl in (1, 0):
        out = half_get(mid, sl) + half_get(yacc, sl) + pb[...]
        xn[sl * SEG : (sl + 1) * SEG, :] = out.astype(bf16)
    hid_cp = remote(xn.at[pl.ds(SEG, SEG)], hid_h.at[y], out_s.at[0], out_r.at[0], far)
    hid_cp.start()
    hid_lo = pltpu.make_async_copy(xn.at[pl.ds(0, SEG)], hid_h.at[y], loc_out.at[0])
    hid_lo.start()

    def do_copy(sl):
        blk = bl if sl == 0 else br
        dst = xn.at[pl.ds(OWN, OWN), pl.ds(aligned(blk * SEG, SEG), SEG)]
        return remote(oTf.at[sl, pl.ds(0, OWN)], dst, d_s.at[sl], d_r.at[sl], sib)

    for sl in (0, 1):
        blk = bl if sl == 0 else br
        rows = slice(sl * SEG, (sl + 1) * SEG)
        gm = cot2[rows, :].astype(f32) + norm_back(half_get(mid, sl), half_get(dxacc, sl) * mg[...])
        half_put(dxacc, sl, gm)
        gmb = gm.astype(bf16)
        oTf[sl, 0:OWN, :] = mm(wout[pl.ds(ow, OWN), :], gmb, 1, 1).astype(bf16)
        do_copy(sl).start()
        xn[OWN:D, pl.ds(aligned(blk * SEG, SEG), SEG)] = mm(wout[pl.ds(cw, OWN), :], gmb, 1, 1).astype(bf16)

    dk = yacc
    dv = mid
    dk[...] = jnp.zeros_like(dk)
    dv[...] = jnp.zeros_like(dv)
    for cp in (do_copy(0), do_copy(1)):
        cp.wait()
    for b in range(NB):
        cols = slice(b * SEG, (b + 1) * SEG)
        li = linv[:, cols]
        dof = xn[OWN:D, cols].astype(f32)
        prod = dof * oTo[b].astype(f32)
        dl = jnp.concatenate(
            [jnp.sum(prod[h * HD : (h + 1) * HD], axis=0, keepdims=True) for h in range(NH)], axis=0
        ) * li
        deltap[:, cols] = dl
        dos = (dof * rep(li, HD)).astype(bf16)
        spread(wproj, cols, dos.T)
        dpp = mm(pvbd[...], dos)
        dsb = (ep[:, cols].astype(f32) * (dpp - rep(dl, PP))).astype(bf16)
        dsp[:, cols] = dsb
        dqT[:, cols] = mm(pkT[...], dsb)

    def prefix_grad(left, right, at):
        for n in range(2):
            t = mm(left, right[0:1024, n * 512 : (n + 1) * 512])
            for p in range(2):
                h = 4 * n + 2 * p
                v = t[h * PP : (h + 1) * PP, 2 * p * 128 : (2 * p + 1) * 128]
                v = v + t[(h + 1) * PP : (h + 2) * PP, (2 * p + 1) * 128 : (2 * p + 2) * 128]
                gpre[:, at + h * HD : at + h * HD + 128] = v

    prefix_grad(dsp[...], qm, 0)
    prefix_grad(ep[...], wproj, OWN)

    def at_tile(i, j):
        qi = jnp.where(y == 1, j, 3 - i)
        ki = jnp.where(y == 1, i, 3 - j)
        return qi, ki

    def tile(i, j):
        qi, ki = at_tile(i, j)
        qr = pl.ds(aligned(qi * SEG, SEG), SEG)
        kr = pl.ds(aligned(ki * SEG, SEG), SEG)
        off = pl.ds(aligned((lax.div(qi * (qi + 1), 2) + ki) * SEG, SEG), SEG)
        for hp in range(4):
            hl = slice(hp * 128, (hp + 1) * 128)
            gk = dk[kr, hl]
            gv = dv[kr, hl]
            for u in range(2):
                h = 2 * hp + u
                hw = slice(h * 128, (h + 1) * 128)
                hrows = slice(h * HD, (h + 1) * HD)
                doh = wproj[qr, hw]
                e = es[h, off, :]
                dp = mm(vx[hp, kr, :], doh, 1, 1)
                ds = (e.astype(f32) * (dp - deltap[h : h + 1, qr])).astype(bf16)
                gv = gv + mm(e, doh)
                gk = gk + mm(ds, qm[qr, hw])
                dqT[hrows, qr] += mm(kT[hrows, kr], ds)
            dk[kr, hl] = gk
            dv[kr, hl] = gv

    def block_at(i):
        return jnp.where(y == 1, i, 3 - i)

    def d_copy(b, i):
        sl = slot_of(b)
        return remote(
            wfc.at[pl.ds(aligned(sl * SEG, SEG), SEG), pl.ds(2048, 1536)],
            wfc.at[pl.ds(aligned((2 * sl + c) * SEG, SEG), SEG), pl.ds(0, 1536)],
            g_s.at[i // 2], g_r.at[i // 2], sib,
        )

    def done_block(i):
        b = block_at(i)
        br_ = pl.ds(aligned(b * SEG, SEG), SEG)
        sl = slot_of(b)
        mine = lax.rem(b, 2) == c
        parts = (
            (dqT[:, br_] * HD ** (-0.5)).astype(bf16).T,
            dk[br_, :].astype(bf16),
            dv[br_, :].astype(bf16),
        )
        row = aligned(jnp.where(mine, 2 * sl + c, sl) * SEG, SEG)
        for p in range(3):
            col = aligned(jnp.where(mine, 0, 2048) + p * 512, 512)
            wfc[pl.ds(row, SEG), pl.ds(col, 512)] = parts[p]

        @pl.when(jnp.logical_not(mine))
        def _():
            d_copy(b, i).start()

    def finish(i):
        b = block_at(i)
        sl = slot_of(b)

        @pl.when(lax.rem(b, 2) == c)
        def _():
            d_copy(b, i).wait_recv()
            acc = None
            for p in range(3):
                for hf in range(2):
                    a = wfc[pl.ds(aligned((2 * sl + hf) * SEG, SEG), SEG), p * 512 : (p + 1) * 512]
                    t = mm(a, wqkv[:, p * D + hf * OWN : p * D + (hf + 1) * OWN], 1, 1)
                    acc = t if acc is None else acc + t
            rows = pl.ds(aligned(sl * SEG, SEG), SEG)
            rows2 = pl.ds(aligned(OWN + sl * SEG, SEG), SEG)
            gm = jnp.concatenate([dxacc[rows, :], dxacc[rows2, :]], axis=1)
            res = gm + norm_back(tok2[rows, :].astype(f32), acc * ag[...])
            xn[rows, :] = res.astype(bf16)
            if i < 2:
                gt_cp().start()
            else:
                gt_lo().start()

    def gt_cp():
        return remote(xn.at[pl.ds(SEG, SEG)], gtok_h.at[y], out_s.at[1], out_r.at[1], far)

    def gt_lo():
        return pltpu.make_async_copy(xn.at[pl.ds(0, SEG)], gtok_h.at[y], loc_out.at[1])

    hid_cp.wait_send()
    hid_lo.wait()
    cot_cp.wait_send()
    for i in range(4):
        lax.fori_loop(i, 4, lambda j, carry, i=i: (tile(i, j), carry)[1], 0)
        done_block(i)
        if i:
            finish(i - 1)
    finish(3)

    for i in range(2):
        pltpu.make_async_copy(
            wfc.at[pl.ds(0, SEG), pl.ds(2048, 1536)], wfc.at[pl.ds(0, SEG), pl.ds(2048, 1536)], g_s.at[i]
        ).wait()
    gt_lo().wait()
    gt_cp().wait()
    hid_cp.wait_recv()


def layer(args):
    vm = pl.BlockSpec(memory_space=pltpu.VMEM)
    hb = pl.BlockSpec(memory_space=pl.ANY)
    sm = pl.BlockSpec(memory_space=pltpu.SMEM)
    (tokens, cotangent, src_len, tgt_len, attn_gain, attn_shift, qkv_weight, qkv_bias, out_weight, out_bias,
     mlp_gain, mlp_shift, fc_weight, fc_bias, proj_weight, proj_bias, embed_rows, mid_weight, mid_bias,
     kv_weight, kv_bias) = args
    V = pltpu.VMEM
    dma = pltpu.SemaphoreType.DMA
    return pl.pallas_call(
        kernel,
        out_shape=(
            jax.ShapeDtypeStruct(tokens.shape, bf16),
            jax.ShapeDtypeStruct(tokens.shape, bf16),
            jax.ShapeDtypeStruct((PP, D), f32),
        ),
        in_specs=[hb, hb, sm, sm] + [vm] * 10 + [hb] * 4 + [vm, hb, hb],
        out_specs=(hb, hb, vm),
        scratch_shapes=[
            V((D, 3 * D), bf16), V((D, D), bf16), V((D, FF), bf16), V((FF, D), bf16),
            V((OWN, D), bf16), V((OWN, D), bf16), V((D, D), bf16), V((D, D), bf16),
            V((4, PP + D, 128), bf16), V((OWN, D), bf16), V((4, D, 128), bf16), V((OWN, D), bf16),
            V((NH, 10 * SEG, SEG), bf16), V((NH * PP, D), bf16), V((NH * PP, D), bf16),
            V((OWN, SEG), f32), V((NB, OWN, SEG), bf16), V((2, D, SEG), bf16),
            V((D, OWN), f32), V((D, OWN), f32), V((D, OWN), f32),
            V((OWN, D), f32), V((PP + D, 128), f32), V((SEG, SEG), f32),
            V((OWN, NH * PP), bf16), V((NH * PP, OWN), bf16), V((OWN, NH * PP), bf16),
            V((NH, D), f32), V((NH, D), f32),
            V((1, D), f32), V((1, D), f32), V((1, 3 * D), f32), V((1, D), f32), V((1, D), f32), V((1, D), f32),
            V((1, FF), f32), V((1, D), f32), V((1, 2 * D), f32),
            dma((10,)), dma((1,)), dma((5,)), dma((5,)), dma((5,)), dma((5,)), dma((2,)), dma((2,)),
            dma((2,)), dma((2,)), dma((2,)), dma((2,)), dma((2,)), dma((2,)), dma((2,)),
        ],
        compiler_params=pltpu.CompilerParams(
            collective_id=0, has_side_effects=True, vmem_limit_bytes=64 << 20
        ),
    )(tokens, cotangent, src_len, tgt_len, attn_gain, attn_shift, qkv_bias, out_bias, mlp_gain, mlp_shift, fc_bias,
      proj_bias, mid_bias, kv_bias, qkv_weight, out_weight, fc_weight, proj_weight, embed_rows, mid_weight, kv_weight)


def reparam_back(grad_prefix, embed_f, midw_f, kvw_f, prefix_hidden):
    grad_kvb = jnp.sum(grad_prefix, axis=0)
    grad_kvw = jnp.dot(prefix_hidden.T, grad_prefix, precision=HIGH)
    grad_pre = jnp.dot(grad_prefix, kvw_f.T, precision=HIGH) * (1.0 - prefix_hidden * prefix_hidden)
    grad_midb = jnp.sum(grad_pre, axis=0)
    grad_midw = jnp.dot(embed_f.T, grad_pre, precision=HIGH)
    grad_embed = jnp.dot(grad_pre, midw_f.T, precision=HIGH)
    return (grad_embed, grad_midw, grad_midb, grad_kvw, grad_kvb)


def on_device(*args):
    embed_rows, mid_weight, mid_bias, kv_weight, kv_bias = args[16:]
    hidden_out, grad_tokens, own = layer(args)
    own = own[:PRE]
    half = lax.rem(lax.axis_index("seq"), 2)
    parts = jnp.where(jnp.arange(2)[None, None, :, None] == half, own.reshape(PRE, 2, 1, OWN), 0.0)
    grad_prefix = lax.psum(parts.reshape(PRE, 2 * D), ("dp", "seq"))
    embed_f = embed_rows.astype(f32)
    midw_f = mid_weight.astype(f32)
    kvw_f = kv_weight.astype(f32)
    prefix_hidden = jnp.tanh(jnp.dot(embed_f, midw_f, precision=HIGH) + mid_bias.astype(f32))
    return (hidden_out, grad_tokens) + reparam_back(grad_prefix, embed_f, midw_f, kvw_f, prefix_hidden)


def solution(mesh):
    split = P("dp", "seq", None)
    return jax.shard_map(
        on_device,
        mesh=mesh,
        in_specs=(split, split, P("dp"), P("dp")) + (P(),) * 17,
        out_specs=(split, split, P(), P(), P(), P(), P()),
        check_vma=False,
    )
```

```python
import functools

import jax
import jax.numpy as jnp
from jax import lax
from jax.experimental import pallas as pl
from jax.experimental.pallas import tpu as pltpu
from jax.sharding import PartitionSpec as P

D = 1024
HD = 64
FF = 4096
PRE = 10
PP = 16
SEG = 256
OWN = 512
NH = 8
NB = 4
NRED = 8
EPS = 1e-05
NEG = -1e30
MESH = pl.DeviceIdType.MESH
f32 = jnp.float32
bf16 = jnp.bfloat16


def mm(a, b, ca=1, cb=0):
    return lax.dot_general(a, b, (((ca,), (cb,)), ((), ())), preferred_element_type=f32)


def centre(v):
    mean = jnp.mean(v, axis=-1, keepdims=True)
    cen = v - mean
    var = jnp.mean(cen * cen, axis=-1, keepdims=True)
    return cen, lax.rsqrt(var + EPS)


def norm_back(v, incoming):
    cen, r = centre(v)
    xhat = cen * r
    m1 = jnp.mean(incoming, axis=-1, keepdims=True)
    m2 = jnp.mean(incoming * xhat, axis=-1, keepdims=True)
    return r * (incoming - m1 - xhat * m2)


def aligned(i, n):
    return pl.multiple_of(i, n)


def split3(v):
    hi = v.astype(bf16)
    rest = v - hi.astype(f32)
    mid = rest.astype(bf16)
    lo = (rest - mid.astype(f32)).astype(bf16)
    return hi, mid, lo


def kernel(
    ndp,
    tok_h, cot_h, src, tgt,
    ag1, ash1, qb1, ob1, mg1, msh1, fb1, pb1, mb1, kvb1,
    wqkv_h, wout_h, wfc_h, wproj_h, emb, midw_h, kvw_h,
    hid_h, gtok_h, gfull, hidden_o,
    wqkv, wout, wfc, wproj,
    tok2, cot2, xn, qm, kx, kT, vx, vT, es, ep, dsp, ot, oTo, oTf,
    mid, yacc, dxacc, dqT, kb, dbias,
    pkT, pvbd, pvT, linv, deltap, gown, rs, red,
    ag, ash, qb, ob, mg, msh, fb, pb, kvb,
    wsem, lsem, far_s, far_r, xn_s, xn_r, o_s, o_r, d_s, d_r, g_s, g_r, out_s, out_r, loc_out,
    p1_s, p1_r, pb_s, pb_r, p2_s, p2_r,
):
    dp = lax.axis_index("dp")
    s = lax.axis_index("seq")
    y = lax.div(s, 2)
    c = lax.rem(s, 2)
    sib = 2 * y + (1 - c)
    far = 2 * (1 - y) + c
    bl = 2 * y + c
    br = 2 * (1 - y) + c
    cw = aligned(c * OWN, OWN)
    ow = aligned((1 - c) * OWN, OWN)

    def load(i, src_ref, dst_ref):
        cp = pltpu.make_async_copy(src_ref, dst_ref, wsem.at[i])
        cp.start()
        return cp

    ld_tok = load(0, tok_h.at[y], tok2.at[pl.ds(0, SEG)])
    ld_mid0 = load(1, midw_h.at[pl.ds(0, 512)], vT.at[:, pl.ds(0, 512)])
    ld_mid1 = load(2, midw_h.at[pl.ds(512, 512)], vT.at[:, pl.ds(512, 512)])
    ld_kvk = load(3, kvw_h.at[:, pl.ds(cw, OWN)], kT.at[:, pl.ds(0, OWN)])
    ld_kvv = load(4, kvw_h.at[:, pl.ds(aligned(D + c * OWN, OWN), OWN)], kT.at[:, pl.ds(OWN, OWN)])
    ld_qkv = load(5, wqkv_h, wqkv)
    ld_cot = load(6, cot_h.at[y], cot2.at[pl.ds(0, SEG)])
    ld_out = load(7, wout_h, wout)
    ld_fc = load(8, wfc_h, wfc)
    ld_proj = load(9, wproj_h, wproj)

    barrier = pltpu.get_barrier_semaphore()
    for peer in (sib, far):
        pl.semaphore_signal(barrier, inc=1, device_id={"seq": peer}, device_id_type=MESH)

    def greet(j, carry):
        @pl.when(j != dp)
        def _():
            pl.semaphore_signal(barrier, inc=1, device_id={"dp": j}, device_id_type=MESH)
        return carry

    lax.fori_loop(0, ndp, greet, 0)
    pl.semaphore_wait(barrier, ndp + 1)

    def remote(src_ref, dst_ref, ss, rs, peer):
        return pltpu.make_async_remote_copy(
            src_ref=src_ref, dst_ref=dst_ref, send_sem=ss, recv_sem=rs,
            device_id={"seq": peer}, device_id_type=MESH,
        )

    CH = 64
    NCH = SEG // CH
    tok_cp = [
        remote(
            tok_h.at[1 - y, pl.ds(j * CH, CH)], tok2.at[pl.ds(SEG + j * CH, CH)],
            far_s.at[j], far_r.at[j], far,
        )
        for j in range(NCH)
    ]
    for cp in tok_cp:
        cp.start()
    cot_cp = remote(cot_h.at[1 - y], cot2.at[pl.ds(SEG, SEG)], far_s.at[NCH], far_r.at[NCH], far)

    for dst, vec in ((ag, ag1), (ash, ash1), (qb, qb1), (ob, ob1), (mg, mg1), (msh, msh1), (fb, fb1), (pb, pb1), (kvb, kvb1)):
        n = vec.shape[0]
        for i in range(0, n, 1024):
            dst[:, i : i + 1024] = vec[pl.ds(i, 1024)].astype(f32).reshape(1, 1024)
    total = src[y] + tgt[y]
    start = src[y]
    rowp = lax.broadcasted_iota(jnp.int32, (PP, 128), 0)
    kb[0:PP, :] = jnp.where(rowp < PRE, 0.0, NEG)
    for b in range(NB):
        pos = lax.broadcasted_iota(jnp.int32, (SEG, 128), 0) + b * SEG
        kb[PP + b * SEG : PP + (b + 1) * SEG, :] = jnp.where(pos < total, 0.0, NEG)

    def norm_rows(row0, n, dst0):
        cen, r = centre(tok2[row0 : row0 + n, :].astype(f32))
        xn[pl.ds(aligned(dst0, n), n), :] = (cen * r * ag[...] + ash[...]).astype(bf16)

    ld_tok.wait()
    norm_rows(0, SEG, bl * SEG)
    xl = xn.at[pl.ds(aligned(bl * SEG, SEG), SEG)]
    xl_cp = remote(xl, xl, xn_s.at[NCH], xn_r.at[NCH], sib)
    xl_cp.start()

    ld_mid0.wait()
    ld_mid1.wait()
    embp = jnp.concatenate([emb[...], jnp.zeros((PP - PRE, D), bf16)], axis=0)
    pre = mm(embp[:, 0:512], vT[:, 0:512]) + mm(embp[:, 512:1024], vT[:, 512:1024])
    pre = pre + mb1[...].astype(f32).reshape(1, 512)
    hidden = jnp.tanh(pre)
    hidden_o[...] = hidden
    ld_kvk.wait()
    ld_kvv.wait()
    h3 = jnp.concatenate(split3(hidden), axis=0)
    pk3 = mm(h3, kT[:, 0:OWN])
    pv3 = mm(h3, kT[:, OWN : 2 * OWN])
    pk = pk3[0:PP] + pk3[PP : 2 * PP] + pk3[2 * PP :] + kvb[:, pl.ds(cw, OWN)]
    pv = pv3[0:PP] + pv3[PP : 2 * PP] + pv3[2 * PP :] + kvb[:, pl.ds(aligned(D + c * OWN, OWN), OWN)]
    for hp in range(4):
        kx[hp, 0:PP, :] = pk[:, hp * 128 : (hp + 1) * 128].astype(bf16)
    hr = lax.broadcasted_iota(jnp.int32, (NH * PP, OWN), 0) // PP
    hc = lax.broadcasted_iota(jnp.int32, (NH * PP, OWN), 1) // HD
    pk8 = jnp.where(hr == hc, jnp.concatenate([pk] * NH, axis=0), 0.0)
    pv8 = jnp.where(hr == hc, jnp.concatenate([pv] * NH, axis=0), 0.0)
    pvbd[...] = pv8.astype(bf16)
    pkT[...] = pk8.T.astype(bf16)
    pvT[...] = pv8.T.astype(bf16)

    lane = lax.broadcasted_iota(jnp.int32, (1, 128), 1)
    lo_half = jnp.where(lane < HD, 1.0, 0.0).astype(bf16)
    hi_half = jnp.where(lane < HD, 0.0, 1.0).astype(bf16)

    def spread(dst, rows, val):
        for hp in range(4):
            pair = val[:, hp * 128 : (hp + 1) * 128]
            dst[rows, 2 * hp * 128 : (2 * hp + 1) * 128] = pair * lo_half
            dst[rows, (2 * hp + 1) * 128 : (2 * hp + 2) * 128] = pair * hi_half

    def project(b):
        rows = pl.ds(aligned(b * SEG, SEG), SEG)
        krows = pl.ds(aligned(PP + b * SEG, PP), SEG)
        x = xn[rows, :]
        q = (mm(x, wqkv[:, pl.ds(cw, OWN)]) + qb[:, pl.ds(cw, OWN)]).astype(bf16) * jnp.asarray(HD ** (-0.5), bf16)
        spread(qm, rows, q)
        kw = pl.ds(aligned(D + c * OWN, OWN), OWN)
        k = (mm(x, wqkv[:, kw]) + qb[:, kw]).astype(bf16)
        kT[:, rows] = k.T
        vw = pl.ds(aligned(2 * D + c * OWN, OWN), OWN)
        v = (mm(x, wqkv[:, vw]) + qb[:, vw]).astype(bf16)
        vT[:, rows] = v.T
        for hp in range(4):
            kx[hp, krows, :] = k[:, hp * 128 : (hp + 1) * 128]
            vx[hp, rows, :] = v[:, hp * 128 : (hp + 1) * 128]

    ld_qkv.wait()
    project(bl)
    xl_cp.wait()
    project(lax.bitwise_xor(bl, 1))

    fw = []
    for j in range(NCH):
        tok_cp[j].wait_recv()
        norm_rows(SEG + j * CH, CH, br * SEG + j * CH)
        xr = xn.at[pl.ds(aligned(br * SEG + j * CH, CH), CH)]
        cp = remote(xr, xr, xn_s.at[j], xn_r.at[j], sib)
        cp.start()
        fw.append(cp)
    for cp in tok_cp:
        cp.wait_send()
    cot_cp.start()
    project(br)
    for cp in fw:
        cp.wait()
    project(lax.bitwise_xor(br, 1))

    def slot_of(b):
        return lax.bitwise_xor(b // 2 if isinstance(b, int) else lax.div(b, 2), y)

    def rep(vals, n):
        return jnp.concatenate([jnp.broadcast_to(vals[h : h + 1], (n, vals.shape[1])) for h in range(NH)], axis=0)

    def twice(v):
        return jnp.concatenate([v, v], axis=1)

    tri = lax.broadcasted_iota(jnp.int32, (SEG, SEG), 0) <= lax.broadcasted_iota(jnp.int32, (SEG, SEG), 1)

    def o_copy(b):
        return remote(
            oTo.at[b], oTf.at[slot_of(b), pl.ds(cw, OWN)], o_s.at[slot_of(b)], o_r.at[slot_of(b)], sib
        )

    for b in (3, 2, 1, 0):
        cols = slice(b * SEG, (b + 1) * SEG)
        low = PP + b * SEG
        off = SEG * (b * (b + 1) // 2)
        dbias[...] = jnp.where(tri, twice(kb[low : low + SEG, :]), NEG)

        def heads(hp, carry, b=b, cols=cols, low=low, off=off):
            for u in range(2):
                h = 2 * hp + u
                qh = qm[cols, pl.ds(aligned(h * 128, 128), 128)]
                s0 = mm(kx[hp, 0:low, :], qh, 1, 1) + twice(kb[0:low, :])
                s1 = mm(kx[hp, low : low + SEG, :], qh, 1, 1) + dbias[...]
                m = jnp.maximum(jnp.max(s0, axis=0, keepdims=True), jnp.max(s1, axis=0, keepdims=True))
                e0 = jnp.exp(s0 - m)
                e1 = jnp.exp(s1 - m)
                den = jnp.sum(e0, axis=0, keepdims=True) + jnp.sum(e1, axis=0, keepdims=True)
                linv[pl.ds(h, 1), cols] = 1.0 / den
                p0 = e0.astype(bf16)
                p1 = e1.astype(bf16)
                ep[pl.ds(aligned(h * PP, PP), PP), cols] = p0[0:PP]
                hrows = pl.ds(aligned(h * HD, HD), HD)
                if b:
                    es[h, off : off + b * SEG, :] = p0[PP:]
                es[h, off + b * SEG : off + (b + 1) * SEG, :] = p1
                ot[hrows, :] = mm(vT[hrows, 0 : (b + 1) * SEG], es[h, off : off + (b + 1) * SEG, :])
            return carry

        lax.fori_loop(0, 4, heads, 0)
        o = (ot[...] + mm(pvT[...], ep[:, cols])) * rep(linv[:, cols], HD)
        oTo[b] = o.astype(bf16)

        @pl.when(c == b % 2)
        def _(b=b):
            oTf[slot_of(b), pl.ds(cw, OWN), :] = oTo[b]

        @pl.when(c != b % 2)
        def _(b=b):
            o_copy(b).start()

    def half_get(ref, sl):
        return jnp.concatenate([ref[sl * SEG : (sl + 1) * SEG, :], ref[OWN + sl * SEG : OWN + (sl + 1) * SEG, :]], axis=1)

    def half_put(ref, sl, val):
        ref[sl * SEG : (sl + 1) * SEG, :] = val[:, 0:OWN]
        ref[OWN + sl * SEG : OWN + (sl + 1) * SEG, :] = val[:, OWN:]

    ld_out.wait()
    ld_cot.wait()
    cot_cp.wait_recv()
    for sl in (0, 1):
        pltpu.make_async_copy(oTf.at[sl, pl.ds(ow, OWN)], oTf.at[sl, pl.ds(ow, OWN)], o_r.at[sl]).wait()
        blk = bl if sl == 0 else br
        m = mm(oTf[sl], wout[...], 0, 0) + ob[...] + tok2[sl * SEG : (sl + 1) * SEG, :].astype(f32)
        half_put(mid, sl, m)
        cen, r = centre(m)
        xn[sl * SEG : (sl + 1) * SEG, :] = (cen * r * mg[...] + msh[...]).astype(bf16)
        pos = lax.broadcasted_iota(jnp.int32, (SEG, 1), 0) + blk * SEG
        seen = jnp.where((pos >= start) & (pos < total), 1.0, 0.0)
        cot2[sl * SEG : (sl + 1) * SEG, :] = (cot2[sl * SEG : (sl + 1) * SEG, :].astype(f32) * seen).astype(bf16)
    for sl in (0, 1):
        pltpu.make_async_copy(oTo.at[sl], oTo.at[sl], o_s.at[sl]).wait()

    ld_fc.wait()
    ld_proj.wait()
    yacc[...] = jnp.zeros_like(yacc)
    dxacc[...] = jnp.zeros_like(dxacc)
    FC = 512

    def feed(i, carry):
        fs = pl.ds(aligned(i * FC, FC), FC)
        u = mm(xn[0:OWN, :], wfc[:, fs]) + fb[:, fs]
        da = mm(cot2[...], wproj[fs, :], 1, 1)
        u2 = u * u
        th = jnp.tanh(u * (0.7978845608028654 + 0.035677408136300125 * u2))
        hh = 0.5 * th + 0.5
        act = u * hh
        slope = hh + act * (1.0 - hh) * (1.5957691216057308 + 0.21406444881780075 * u2)
        ab = act.astype(bf16)
        db = (slope * da).astype(bf16)
        for n in range(2):
            rows = slice(n * OWN, (n + 1) * OWN)
            yacc[rows, :] += mm(ab, wproj[fs, rows])
            dxacc[rows, :] += mm(db, wfc[rows, fs], 1, 1)
        return carry

    lax.fori_loop(0, FF // FC, feed, 0)

    for sl in (1, 0):
        out = half_get(mid, sl) + half_get(yacc, sl) + pb[...]
        xn[sl * SEG : (sl + 1) * SEG, :] = out.astype(bf16)
    hid_cp = remote(xn.at[pl.ds(SEG, SEG)], hid_h.at[y], out_s.at[0], out_r.at[0], far)
    hid_cp.start()
    hid_lo = pltpu.make_async_copy(xn.at[pl.ds(0, SEG)], hid_h.at[y], loc_out.at[0])
    hid_lo.start()

    def do_copy(sl):
        blk = bl if sl == 0 else br
        dst = xn.at[pl.ds(OWN, OWN), pl.ds(aligned(blk * SEG, SEG), SEG)]
        return remote(oTf.at[sl, pl.ds(0, OWN)], dst, d_s.at[sl], d_r.at[sl], sib)

    for sl in (0, 1):
        blk = bl if sl == 0 else br
        rows = slice(sl * SEG, (sl + 1) * SEG)
        gm = cot2[rows, :].astype(f32) + norm_back(half_get(mid, sl), half_get(dxacc, sl) * mg[...])
        half_put(dxacc, sl, gm)
        gmb = gm.astype(bf16)
        oTf[sl, 0:OWN, :] = mm(wout[pl.ds(ow, OWN), :], gmb, 1, 1).astype(bf16)
        do_copy(sl).start()
        xn[OWN:D, pl.ds(aligned(blk * SEG, SEG), SEG)] = mm(wout[pl.ds(cw, OWN), :], gmb, 1, 1).astype(bf16)

    dk = yacc
    dv = mid
    dk[...] = jnp.zeros_like(dk)
    dv[...] = jnp.zeros_like(dv)
    for cp in (do_copy(0), do_copy(1)):
        cp.wait()
    for b in range(NB):
        cols = slice(b * SEG, (b + 1) * SEG)
        li = linv[:, cols]
        dof = xn[OWN:D, cols].astype(f32)
        prod = dof * oTo[b].astype(f32)
        dl = jnp.concatenate(
            [jnp.sum(prod[h * HD : (h + 1) * HD], axis=0, keepdims=True) for h in range(NH)], axis=0
        ) * li
        deltap[:, cols] = dl
        dos = (dof * rep(li, HD)).astype(bf16)
        spread(wproj, cols, dos.T)
        dpp = mm(pvbd[...], dos)
        dsb = (ep[:, cols].astype(f32) * (dpp - rep(dl, PP))).astype(bf16)
        dsp[:, cols] = dsb
        dqT[:, cols] = mm(pkT[...], dsb)

    def prefix_grad(left, right, at):
        for n in range(2):
            t = mm(left, right[0:1024, n * 512 : (n + 1) * 512])
            for p in range(2):
                h = 4 * n + 2 * p
                v = t[h * PP : (h + 1) * PP, 2 * p * 128 : (2 * p + 1) * 128]
                v = v + t[(h + 1) * PP : (h + 2) * PP, (2 * p + 1) * 128 : (2 * p + 2) * 128]
                gown[at + h // 2] = v

    prefix_grad(dsp[...], qm, 0)
    prefix_grad(ep[...], wproj, NRED // 2)

    def across(src_ref, dst_ref, ss, rsm, j):
        return pltpu.make_async_remote_copy(
            src_ref=src_ref, dst_ref=dst_ref, send_sem=ss, recv_sem=rsm, device_id={"dp": j}, device_id_type=MESH
        )

    def others(n, fn):
        def step(j, carry):
            @pl.when(j != dp)
            def _():
                fn(j)
            return carry

        lax.fori_loop(0, n, step, 0)

    mychunk = c * NRED + dp

    def p1_copy(j):
        return across(gown.at[j], rs.at[dp], p1_s.at[j], p1_r.at[dp], j)

    def p1_back(j):
        return across(gown.at[0], rs.at[j], p1_s.at[0], p1_r.at[j], j)

    def p2_copy(j):
        return across(gfull.at[mychunk], gfull.at[mychunk], p2_s.at[j], p2_r.at[dp], j)

    def p2_back(j):
        return across(gfull.at[0], gfull.at[c * NRED + j], p2_s.at[0], p2_r.at[j], j)

    def pb_copy():
        return remote(red.at[0], red.at[1], pb_s.at[0], pb_r.at[0], far)

    def pc_copy():
        mine = gfull.at[pl.ds(c * NRED, NRED)]
        return remote(mine, mine, pb_s.at[1], pb_r.at[1], sib)

    def prefix_sum(stage):
        if stage == 0:
            others(NRED, lambda j: p1_copy(j).start())

            @pl.when(dp < NRED)
            def _():
                rs[dp] = gown[dp]
        elif stage == 1:
            @pl.when(dp < NRED)
            def _():
                others(ndp, lambda j: p1_back(j).wait_recv())
                red[0] = lax.fori_loop(1, ndp, lambda j, a: a + rs[j], rs[0])
                pb_copy().start()
        elif stage == 2:
            @pl.when(dp < NRED)
            def _():
                pb_copy().wait()
                gfull[mychunk] = red[0] + red[1]
                others(ndp, lambda j: p2_copy(j).start())
        elif stage == 3:
            others(NRED, lambda j: p2_back(j).wait_recv())
            pc_copy().start()
        else:
            pc_copy().wait()
            others(NRED, lambda j: p1_copy(j).wait_send())

            @pl.when(dp < NRED)
            def _():
                others(ndp, lambda j: p2_copy(j).wait_send())

    prefix_sum(0)

    def at_tile(i, j):
        qi = jnp.where(y == 1, j, 3 - i)
        ki = jnp.where(y == 1, i, 3 - j)
        return qi, ki

    def tile(i, j):
        qi, ki = at_tile(i, j)
        qr = pl.ds(aligned(qi * SEG, SEG), SEG)
        kr = pl.ds(aligned(ki * SEG, SEG), SEG)
        off = pl.ds(aligned((lax.div(qi * (qi + 1), 2) + ki) * SEG, SEG), SEG)
        for hp in range(4):
            hl = slice(hp * 128, (hp + 1) * 128)
            gk = dk[kr, hl]
            gv = dv[kr, hl]
            for u in range(2):
                h = 2 * hp + u
                hw = slice(h * 128, (h + 1) * 128)
                hrows = slice(h * HD, (h + 1) * HD)
                doh = wproj[qr, hw]
                e = es[h, off, :]
                dp = mm(vx[hp, kr, :], doh, 1, 1)
                ds = (e.astype(f32) * (dp - deltap[h : h + 1, qr])).astype(bf16)
                gv = gv + mm(e, doh)
                gk = gk + mm(ds, qm[qr, hw])
                dqT[hrows, qr] += mm(kT[hrows, kr], ds)
            dk[kr, hl] = gk
            dv[kr, hl] = gv

    def block_at(i):
        return jnp.where(y == 1, i, 3 - i)

    def d_copy(b, i):
        sl = slot_of(b)
        return remote(
            wfc.at[pl.ds(aligned(sl * SEG, SEG), SEG), pl.ds(2048, 1536)],
            wfc.at[pl.ds(aligned((2 * sl + c) * SEG, SEG), SEG), pl.ds(0, 1536)],
            g_s.at[i // 2], g_r.at[i // 2], sib,
        )

    def done_block(i):
        b = block_at(i)
        br_ = pl.ds(aligned(b * SEG, SEG), SEG)
        sl = slot_of(b)
        mine = lax.rem(b, 2) == c
        parts = (
            (dqT[:, br_] * HD ** (-0.5)).astype(bf16).T,
            dk[br_, :].astype(bf16),
            dv[br_, :].astype(bf16),
        )
        row = aligned(jnp.where(mine, 2 * sl + c, sl) * SEG, SEG)
        for p in range(3):
            col = aligned(jnp.where(mine, 0, 2048) + p * 512, 512)
            wfc[pl.ds(row, SEG), pl.ds(col, 512)] = parts[p]

        @pl.when(jnp.logical_not(mine))
        def _():
            d_copy(b, i).start()

    def finish(i):
        b = block_at(i)
        sl = slot_of(b)

        @pl.when(lax.rem(b, 2) == c)
        def _():
            d_copy(b, i).wait_recv()
            acc = None
            for p in range(3):
                for hf in range(2):
                    a = wfc[pl.ds(aligned((2 * sl + hf) * SEG, SEG), SEG), p * 512 : (p + 1) * 512]
                    t = mm(a, wqkv[:, p * D + hf * OWN : p * D + (hf + 1) * OWN], 1, 1)
                    acc = t if acc is None else acc + t
            rows = pl.ds(aligned(sl * SEG, SEG), SEG)
            rows2 = pl.ds(aligned(OWN + sl * SEG, SEG), SEG)
            gm = jnp.concatenate([dxacc[rows, :], dxacc[rows2, :]], axis=1)
            res = gm + norm_back(tok2[rows, :].astype(f32), acc * ag[...])
            xn[rows, :] = res.astype(bf16)
            if i < 2:
                gt_cp().start()
            else:
                gt_lo().start()

    def gt_cp():
        return remote(xn.at[pl.ds(SEG, SEG)], gtok_h.at[y], out_s.at[1], out_r.at[1], far)

    def gt_lo():
        return pltpu.make_async_copy(xn.at[pl.ds(0, SEG)], gtok_h.at[y], loc_out.at[1])

    hid_cp.wait_send()
    hid_lo.wait()
    cot_cp.wait_send()
    for i in range(4):
        lax.fori_loop(i, 4, lambda j, carry, i=i: (tile(i, j), carry)[1], 0)
        done_block(i)
        if i < 3:
            prefix_sum(i + 1)
        if i:
            finish(i - 1)
    finish(3)
    prefix_sum(4)

    for i in range(2):
        pltpu.make_async_copy(
            wfc.at[pl.ds(0, SEG), pl.ds(2048, 1536)], wfc.at[pl.ds(0, SEG), pl.ds(2048, 1536)], g_s.at[i]
        ).wait()
    gt_lo().wait()
    gt_cp().wait()
    hid_cp.wait_recv()


def layer(args, ndp):
    vm = pl.BlockSpec(memory_space=pltpu.VMEM)
    hb = pl.BlockSpec(memory_space=pl.ANY)
    sm = pl.BlockSpec(memory_space=pltpu.SMEM)
    (tokens, cotangent, src_len, tgt_len, attn_gain, attn_shift, qkv_weight, qkv_bias, out_weight, out_bias,
     mlp_gain, mlp_shift, fc_weight, fc_bias, proj_weight, proj_bias, embed_rows, mid_weight, mid_bias,
     kv_weight, kv_bias) = args
    V = pltpu.VMEM
    dma = pltpu.SemaphoreType.DMA
    return pl.pallas_call(
        functools.partial(kernel, ndp),
        out_shape=(
            jax.ShapeDtypeStruct(tokens.shape, bf16),
            jax.ShapeDtypeStruct(tokens.shape, bf16),
            jax.ShapeDtypeStruct((2 * NRED, PP, 128), f32),
            jax.ShapeDtypeStruct((PP, 512), f32),
        ),
        in_specs=[hb, hb, sm, sm] + [vm] * 10 + [hb] * 4 + [vm, hb, hb],
        out_specs=(hb, hb, vm, vm),
        scratch_shapes=[
            V((D, 3 * D), bf16), V((D, D), bf16), V((D, FF), bf16), V((FF, D), bf16),
            V((OWN, D), bf16), V((OWN, D), bf16), V((D, D), bf16), V((D, D), bf16),
            V((4, PP + D, 128), bf16), V((OWN, D), bf16), V((4, D, 128), bf16), V((OWN, D), bf16),
            V((NH, 10 * SEG, SEG), bf16), V((NH * PP, D), bf16), V((NH * PP, D), bf16),
            V((OWN, SEG), f32), V((NB, OWN, SEG), bf16), V((2, D, SEG), bf16),
            V((D, OWN), f32), V((D, OWN), f32), V((D, OWN), f32),
            V((OWN, D), f32), V((PP + D, 128), f32), V((SEG, SEG), f32),
            V((OWN, NH * PP), bf16), V((NH * PP, OWN), bf16), V((OWN, NH * PP), bf16),
            V((NH, D), f32), V((NH, D), f32),
            V((NRED, PP, 128), f32), V((ndp, PP, 128), f32), V((2, PP, 128), f32),
            V((1, D), f32), V((1, D), f32), V((1, 3 * D), f32), V((1, D), f32), V((1, D), f32), V((1, D), f32),
            V((1, FF), f32), V((1, D), f32), V((1, 2 * D), f32),
            dma((10,)), dma((1,)), dma((5,)), dma((5,)), dma((5,)), dma((5,)), dma((2,)), dma((2,)),
            dma((2,)), dma((2,)), dma((2,)), dma((2,)), dma((2,)), dma((2,)), dma((2,)),
            dma((NRED,)), dma((ndp,)), dma((2,)), dma((2,)), dma((ndp,)), dma((NRED,)),
        ],
        compiler_params=pltpu.CompilerParams(
            collective_id=0, has_side_effects=True, vmem_limit_bytes=64 << 20
        ),
    )(tokens, cotangent, src_len, tgt_len, attn_gain, attn_shift, qkv_bias, out_bias, mlp_gain, mlp_shift, fc_bias,
      proj_bias, mid_bias, kv_bias, qkv_weight, out_weight, fc_weight, proj_weight, embed_rows, mid_weight, kv_weight)


def reparam_kernel(
    hid_i, gtok_i, gfull, hidden, emb, midw_h, kvw_h,
    hid_o, gtok_o, gemb, gmidw_o, gmidb, gkvw_o, gkvb,
    midw, kvw, gkvw, gmidw, sem,
):
    def go(i, a, b):
        cp = pltpu.make_async_copy(a, b, sem.at[i])
        cp.start()
        return cp

    ld_kv = go(0, kvw_h, kvw)
    ld_mid = go(1, midw_h, midw)
    moves = [go(2, hid_i, hid_o), go(3, gtok_i, gtok_o)]
    quarter = NRED // 2
    order = [half * NRED + part * quarter + j for part in (0, 1) for half in (0, 1) for j in range(quarter)]
    grad = jnp.concatenate([gfull[i] for i in order], axis=1)
    hid = hidden[...]
    h0, h1, h2 = split3(hid)
    g0, g1, g2 = split3(grad)
    left = jnp.concatenate([h0, h1, h0, h1, h2, h0], axis=0)
    right = jnp.concatenate([g0, g0, g1, g1, g0, g2], axis=0)
    W = 512
    for n in range(2 * D // W):
        gkvw[:, n * W : (n + 1) * W] = mm(left, right[:, n * W : (n + 1) * W], 0, 0)
        moves.append(go(4 + n, gkvw.at[:, pl.ds(n * W, W)], gkvw_o.at[:, pl.ds(n * W, W)]))
    gkvb[...] = jnp.sum(grad, axis=0, keepdims=True).reshape(2 * D)
    ld_kv.wait()
    three = mm(jnp.concatenate([g0, g1, g2], axis=0), kvw[...], 1, 1)
    gp = (three[0:PP] + three[PP : 2 * PP] + three[2 * PP :]) * (1.0 - hid * hid)
    gmidb[...] = jnp.sum(gp, axis=0, keepdims=True).reshape(512)
    p0, p1, p2 = split3(gp)
    p3 = jnp.concatenate([p0, p1, p2], axis=0)
    embp = jnp.concatenate([emb[...], jnp.zeros((PP - PRE, D), bf16)], axis=0)
    emb3 = jnp.concatenate([embp] * 3, axis=0)
    gmidw[...] = mm(emb3, p3, 0, 0)
    moves.append(go(8, gmidw, gmidw_o))
    ld_mid.wait()
    back = mm(p3, midw[...], 1, 1)
    gemb[...] = (back[0:PP] + back[PP : 2 * PP] + back[2 * PP :])[0:PRE]
    for cp in moves:
        cp.wait()


def on_device(ndp, *args):
    embed_rows, mid_weight, _, kv_weight, _ = args[16:]
    hidden_out, grad_tokens, gfull, hidden = layer(args, ndp)
    vm = pl.BlockSpec(memory_space=pltpu.VMEM)
    hb = pl.BlockSpec(memory_space=pl.ANY)
    sds = jax.ShapeDtypeStruct
    return pl.pallas_call(
        reparam_kernel,
        out_shape=(
            sds(hidden_out.shape, bf16), sds(grad_tokens.shape, bf16), sds((PRE, D), f32), sds((D, 512), f32),
            sds((512,), f32), sds((512, 2 * D), f32), sds((2 * D,), f32),
        ),
        in_specs=[hb, hb, vm, vm, vm, hb, hb],
        out_specs=(hb, hb, vm, hb, vm, hb, vm),
        scratch_shapes=[
            pltpu.VMEM((D, 512), bf16), pltpu.VMEM((512, 2 * D), bf16), pltpu.VMEM((512, 2 * D), f32),
            pltpu.VMEM((D, 512), f32), pltpu.SemaphoreType.DMA((9,)),
        ],
        compiler_params=pltpu.CompilerParams(vmem_limit_bytes=32 << 20),
    )(hidden_out, grad_tokens, gfull, hidden, embed_rows, mid_weight, kv_weight)


def solution(mesh):
    split = P("dp", "seq", None)
    return jax.shard_map(
        functools.partial(on_device, mesh.shape["dp"]),
        mesh=mesh,
        in_specs=(split, split, P("dp"), P("dp")) + (P(),) * 17,
        out_specs=(split, split, P(), P(), P(), P(), P()),
        check_vma=False,
    )
```

```python
import functools

import jax
import jax.numpy as jnp
from jax import lax
from jax.experimental import pallas as pl
from jax.experimental.pallas import tpu as pltpu
from jax.sharding import PartitionSpec as P

D = 1024
HD = 64
FF = 4096
PRE = 10
PP = 16
SEG = 256
OWN = 512
NH = 8
NB = 4
NRED = 8
VR = 80
EPS = 1e-05
NEG = -1e30
MESH = pl.DeviceIdType.MESH
f32 = jnp.float32
bf16 = jnp.bfloat16


def mm(a, b, ca=1, cb=0):
    return lax.dot_general(a, b, (((ca,), (cb,)), ((), ())), preferred_element_type=f32)


def centre(v):
    mean = jnp.mean(v, axis=-1, keepdims=True)
    cen = v - mean
    var = jnp.mean(cen * cen, axis=-1, keepdims=True)
    return cen, lax.rsqrt(var + EPS)


def norm_back(v, incoming):
    cen, r = centre(v)
    xhat = cen * r
    m1 = jnp.mean(incoming, axis=-1, keepdims=True)
    m2 = jnp.mean(incoming * xhat, axis=-1, keepdims=True)
    return r * (incoming - m1 - xhat * m2)


def aligned(i, n):
    return pl.multiple_of(i, n)


def split3(v):
    hi = v.astype(bf16)
    rest = v - hi.astype(f32)
    mid = rest.astype(bf16)
    lo = (rest - mid.astype(f32)).astype(bf16)
    return hi, mid, lo


def kernel(
    ndp,
    tok_h, cot_h, src, tgt,
    ag1, ash1, qb1, ob1, mg1, msh1, fb1, pb1, mb1, kvb1,
    wqkv_h, wout_h, wfc_h, wproj_h, emb, midw_h, kvw_h,
    hid_h, gtok_h, gfull, hidden_o,
    wqkv, wout, wfc, wproj,
    tok2, cot2, xn, qm, kx, kT, vx, vT, es, ep, dsp, ot, oTo, oTf,
    mid, yacc, dxacc, dqT, kb, dbias,
    pkT, pvbd, pvT, pc0, pc1, linv, deltap, gown, rs, red,
    ag, ash, qb, ob, mg, msh, fb, pb, kvb,
    wsem, far_s, far_r, xn_s, xn_r, o_s, o_r, d_s, d_r, g_s, g_r, out_s, out_r, loc_out,
    p1_s, p1_r, pb_s, pb_r, p2_s, p2_r,
):
    dp = lax.axis_index("dp")
    s = lax.axis_index("seq")
    y = lax.div(s, 2)
    c = lax.rem(s, 2)
    sib = 2 * y + (1 - c)
    far = 2 * (1 - y) + c
    bl = 2 * y + c
    br = 2 * (1 - y) + c
    cw = aligned(c * OWN, OWN)
    ow = aligned((1 - c) * OWN, OWN)

    def load(i, src_ref, dst_ref):
        cp = pltpu.make_async_copy(src_ref, dst_ref, wsem.at[i])
        cp.start()
        return cp

    ld_tok = load(0, tok_h.at[y], tok2.at[pl.ds(0, SEG)])
    ld_mid0 = load(1, midw_h.at[pl.ds(0, 512)], vT.at[pl.ds(0, 512), pl.ds(0, 512)])
    ld_mid1 = load(2, midw_h.at[pl.ds(512, 512)], vT.at[pl.ds(0, 512), pl.ds(512, 512)])
    ld_kvk = load(3, kvw_h.at[:, pl.ds(cw, OWN)], kT.at[:, pl.ds(0, OWN)])
    ld_kvv = load(4, kvw_h.at[:, pl.ds(aligned(D + c * OWN, OWN), OWN)], kT.at[:, pl.ds(OWN, OWN)])

    barrier = pltpu.get_barrier_semaphore()
    for peer in (sib, far):
        pl.semaphore_signal(barrier, inc=1, device_id={"seq": peer}, device_id_type=MESH)

    def greet(j, carry):
        @pl.when(j != dp)
        def _():
            pl.semaphore_signal(barrier, inc=1, device_id={"dp": j}, device_id_type=MESH)
        return carry

    lax.fori_loop(0, ndp, greet, 0)
    pl.semaphore_wait(barrier, ndp + 1)

    def remote(src_ref, dst_ref, ss, rs, peer):
        return pltpu.make_async_remote_copy(
            src_ref=src_ref, dst_ref=dst_ref, send_sem=ss, recv_sem=rs,
            device_id={"seq": peer}, device_id_type=MESH,
        )

    CH = 64
    NCH = SEG // CH
    tok_cp = [
        remote(
            tok_h.at[1 - y, pl.ds(j * CH, CH)], tok2.at[pl.ds(SEG + j * CH, CH)],
            far_s.at[j], far_r.at[j], far,
        )
        for j in range(NCH)
    ]
    for cp in tok_cp:
        cp.start()
    ld_qkv = load(5, wqkv_h, wqkv)
    cot_cp = remote(cot_h.at[1 - y], cot2.at[pl.ds(SEG, SEG)], far_s.at[NCH], far_r.at[NCH], far)

    for dst, vec in ((ag, ag1), (ash, ash1), (qb, qb1), (ob, ob1), (mg, mg1), (msh, msh1), (fb, fb1), (pb, pb1), (kvb, kvb1)):
        n = vec.shape[0]
        for i in range(0, n, 1024):
            dst[:, i : i + 1024] = vec[pl.ds(i, 1024)].astype(f32).reshape(1, 1024)
    total = src[y] + tgt[y]
    start = src[y]
    rowp = lax.broadcasted_iota(jnp.int32, (PP, 128), 0)
    kb[0:PP, :] = jnp.where(rowp < PRE, 0.0, NEG)
    for b in range(NB):
        pos = lax.broadcasted_iota(jnp.int32, (SEG, 128), 0) + b * SEG
        kb[PP + b * SEG : PP + (b + 1) * SEG, :] = jnp.where(pos < total, 0.0, NEG)

    def norm_rows(row0, n, dst0):
        cen, r = centre(tok2[row0 : row0 + n, :].astype(f32))
        xn[pl.ds(aligned(dst0, n), n), :] = (cen * r * ag[...] + ash[...]).astype(bf16)

    ld_tok.wait()
    norm_rows(0, SEG, bl * SEG)
    xl = xn.at[pl.ds(aligned(bl * SEG, SEG), SEG)]
    xl_cp = remote(xl, xl, xn_s.at[NCH], xn_r.at[NCH], sib)
    xl_cp.start()
    ld_cot = load(6, cot_h.at[y], cot2.at[pl.ds(0, SEG)])
    ld_out = load(7, wout_h, wout)

    ld_mid0.wait()
    ld_mid1.wait()
    embp = jnp.concatenate([emb[...], jnp.zeros((PP - PRE, D), bf16)], axis=0)
    pre = mm(embp[:, 0:512], vT[0:512, 0:512]) + mm(embp[:, 512:1024], vT[0:512, 512:1024])
    pre = pre + mb1[...].astype(f32).reshape(1, 512)
    hidden = jnp.tanh(pre)
    hidden_o[...] = hidden
    ld_kvk.wait()
    ld_kvv.wait()
    h3 = jnp.concatenate(split3(hidden), axis=0)
    pk3 = mm(h3, kT[:, 0:OWN])
    pv3 = mm(h3, kT[:, OWN : 2 * OWN])
    pk = pk3[0:PP] + pk3[PP : 2 * PP] + pk3[2 * PP :] + kvb[:, pl.ds(cw, OWN)]
    pv = pv3[0:PP] + pv3[PP : 2 * PP] + pv3[2 * PP :] + kvb[:, pl.ds(aligned(D + c * OWN, OWN), OWN)]
    for hp in range(4):
        kx[hp, 0:PP, :] = pk[:, hp * 128 : (hp + 1) * 128].astype(bf16)
    hr = lax.broadcasted_iota(jnp.int32, (NH * PP, OWN), 0) // PP
    hc = lax.broadcasted_iota(jnp.int32, (NH * PP, OWN), 1) // HD
    pk8 = jnp.where(hr == hc, jnp.concatenate([pk] * NH, axis=0), 0.0)
    pv8 = jnp.where(hr == hc, jnp.concatenate([pv] * NH, axis=0), 0.0)
    pvbd[...] = pv8.astype(bf16)
    pkT[...] = pk8.T.astype(bf16)
    one_t = jnp.where(lax.broadcasted_iota(jnp.int32, (VR - HD, D), 0) == 0, 1.0, 0.0).astype(bf16)
    pv_t = pv8.T
    up = lax.broadcasted_iota(jnp.int32, (VR - HD, NH * PP), 0)
    for h in range(NH):
        here = lax.broadcasted_iota(jnp.int32, (VR - HD, NH * PP), 1) // PP == h
        vT[h * VR + HD : (h + 1) * VR, :] = one_t
        pvT[h * VR : h * VR + HD, :] = pv_t[h * HD : (h + 1) * HD].astype(bf16)
        pvT[h * VR + HD : (h + 1) * VR, :] = jnp.where(here & (up == 0), 1.0, 0.0).astype(bf16)

    lane = lax.broadcasted_iota(jnp.int32, (1, 128), 1)
    lo_half = jnp.where(lane < HD, 1.0, 0.0).astype(bf16)
    hi_half = jnp.where(lane < HD, 0.0, 1.0).astype(bf16)

    def spread(dst, rows, val):
        for hp in range(4):
            pair = val[:, hp * 128 : (hp + 1) * 128]
            dst[rows, 2 * hp * 128 : (2 * hp + 1) * 128] = pair * lo_half
            dst[rows, (2 * hp + 1) * 128 : (2 * hp + 2) * 128] = pair * hi_half

    def project(b):
        rows = pl.ds(aligned(b * SEG, SEG), SEG)
        krows = pl.ds(aligned(PP + b * SEG, PP), SEG)
        x = xn[rows, :]
        q = (mm(x, wqkv[:, pl.ds(cw, OWN)]) + qb[:, pl.ds(cw, OWN)]).astype(bf16) * jnp.asarray(HD ** (-0.5), bf16)
        spread(qm, rows, q)
        kw = pl.ds(aligned(D + c * OWN, OWN), OWN)
        k = (mm(x, wqkv[:, kw]) + qb[:, kw]).astype(bf16)
        kT[:, rows] = k.T
        vw = pl.ds(aligned(2 * D + c * OWN, OWN), OWN)
        v = (mm(x, wqkv[:, vw]) + qb[:, vw]).astype(bf16)
        vt = v.T
        for h in range(NH):
            vT[h * VR : h * VR + HD, rows] = vt[h * HD : (h + 1) * HD]
        for hp in range(4):
            kx[hp, krows, :] = k[:, hp * 128 : (hp + 1) * 128]
            vx[hp, rows, :] = v[:, hp * 128 : (hp + 1) * 128]

    ld_qkv.wait()
    project(bl)
    xl_cp.wait()
    project(lax.bitwise_xor(bl, 1))

    fw = []
    ld_ffn = []
    for j in range(NCH):
        tok_cp[j].wait_recv()
        norm_rows(SEG + j * CH, CH, br * SEG + j * CH)
        xr = xn.at[pl.ds(aligned(br * SEG + j * CH, CH), CH)]
        cp = remote(xr, xr, xn_s.at[j], xn_r.at[j], sib)
        cp.start()
        fw.append(cp)
        if j < 2:
            half = pl.ds(j * OWN, OWN)
            ld_ffn.append(load(8 + j, wfc_h.at[half], wfc.at[half]))
        else:
            half = pl.ds((j - 2) * 2 * D, 2 * D)
            ld_ffn.append(load(8 + j, wproj_h.at[half], wproj.at[half]))
    for cp in tok_cp:
        cp.wait_send()
    cot_cp.start()
    project(br)
    for cp in fw:
        cp.wait()
    project(lax.bitwise_xor(br, 1))

    def slot_of(b):
        return lax.bitwise_xor(b // 2 if isinstance(b, int) else lax.div(b, 2), y)

    def rep(vals, n):
        return jnp.concatenate([jnp.broadcast_to(vals[h : h + 1], (n, vals.shape[1])) for h in range(NH)], axis=0)

    def twice(v):
        return jnp.concatenate([v, v], axis=1)

    tri = lax.broadcasted_iota(jnp.int32, (SEG, SEG), 0) <= lax.broadcasted_iota(jnp.int32, (SEG, SEG), 1)

    def o_copy(b):
        return remote(
            oTo.at[b], oTf.at[slot_of(b), pl.ds(cw, OWN)], o_s.at[slot_of(b)], o_r.at[slot_of(b)], sib
        )

    scs = ((yacc, pc0), (dxacc, pc1))
    for b in (3, 2, 1, 0):
        cols = slice(b * SEG, (b + 1) * SEG)
        low = PP + b * SEG
        off = SEG * (b * (b + 1) // 2)
        dbias[...] = jnp.where(tri, twice(kb[low : low + SEG, :]), NEG)

        width = (b + 1) * SEG

        def stage_a(h):
            sc, pc = scs[h % 2]
            qh = qm[cols, h * 128 : (h + 1) * 128]
            s0 = mm(kx[h // 2, 0:low, :], qh, 1, 1) + twice(kb[0:low, :])
            pc[...] = s0[0:PP]
            if b:
                sc[0 : b * SEG, 0:SEG] = s0[PP:]
            sc[b * SEG : width, 0:SEG] = mm(kx[h // 2, low : low + SEG, :], qh, 1, 1) + dbias[...]

        def stage_b(h):
            sc, pc = scs[h % 2]
            m = jnp.maximum(
                jnp.max(sc[0:width, 0:SEG], axis=0, keepdims=True), jnp.max(pc[...], axis=0, keepdims=True)
            )
            ep[h * PP : (h + 1) * PP, cols] = jnp.exp(pc[...] - m).astype(bf16)
            es[h, off : off + width, :] = jnp.exp(sc[0:width, 0:SEG] - m).astype(bf16)

        def stage_c(h):
            ot[h * VR : (h + 1) * VR, :] = mm(vT[h * VR : (h + 1) * VR, 0:width], es[h, off : off + width, :])

        stage_a(0)
        for h in range(NH):
            if h + 1 < NH:
                stage_a(h + 1)
            if h:
                stage_c(h - 1)
            stage_b(h)
        stage_c(NH - 1)
        o = ot[...] + mm(pvT[...], ep[:, cols])
        for h in range(NH):
            inv = 1.0 / o[h * VR + HD : h * VR + HD + 1]
            linv[h : h + 1, cols] = inv
            oTo[b, h * HD : (h + 1) * HD, :] = (o[h * VR : h * VR + HD] * inv).astype(bf16)

        @pl.when(c == b % 2)
        def _(b=b):
            oTf[slot_of(b), pl.ds(cw, OWN), :] = oTo[b]

        @pl.when(c != b % 2)
        def _(b=b):
            o_copy(b).start()

    def half_get(ref, sl):
        return jnp.concatenate([ref[sl * SEG : (sl + 1) * SEG, :], ref[OWN + sl * SEG : OWN + (sl + 1) * SEG, :]], axis=1)

    def half_put(ref, sl, val):
        ref[sl * SEG : (sl + 1) * SEG, :] = val[:, 0:OWN]
        ref[OWN + sl * SEG : OWN + (sl + 1) * SEG, :] = val[:, OWN:]

    ld_out.wait()
    ld_cot.wait()
    cot_cp.wait_recv()
    for sl in (0, 1):
        pltpu.make_async_copy(oTf.at[sl, pl.ds(ow, OWN)], oTf.at[sl, pl.ds(ow, OWN)], o_r.at[sl]).wait()
        blk = bl if sl == 0 else br
        m = mm(oTf[sl], wout[...], 0, 0) + ob[...] + tok2[sl * SEG : (sl + 1) * SEG, :].astype(f32)
        half_put(mid, sl, m)
        cen, r = centre(m)
        xn[sl * SEG : (sl + 1) * SEG, :] = (cen * r * mg[...] + msh[...]).astype(bf16)
        pos = lax.broadcasted_iota(jnp.int32, (SEG, 1), 0) + blk * SEG
        seen = jnp.where((pos >= start) & (pos < total), 1.0, 0.0)
        cot2[sl * SEG : (sl + 1) * SEG, :] = (cot2[sl * SEG : (sl + 1) * SEG, :].astype(f32) * seen).astype(bf16)
    for sl in (0, 1):
        pltpu.make_async_copy(oTo.at[sl], oTo.at[sl], o_s.at[sl]).wait()

    for cp in ld_ffn:
        cp.wait()
    yacc[...] = jnp.zeros_like(yacc)
    dxacc[...] = jnp.zeros_like(dxacc)
    FC = 512

    def feed(i, carry):
        fs = pl.ds(aligned(i * FC, FC), FC)
        u = mm(xn[0:OWN, :], wfc[:, fs]) + fb[:, fs]
        da = mm(cot2[...], wproj[fs, :], 1, 1)
        u2 = u * u
        th = jnp.tanh(u * (0.7978845608028654 + 0.035677408136300125 * u2))
        hh = 0.5 * th + 0.5
        act = u * hh
        slope = hh + act * (1.0 - hh) * (1.5957691216057308 + 0.21406444881780075 * u2)
        ab = act.astype(bf16)
        db = (slope * da).astype(bf16)
        for n in range(2):
            rows = slice(n * OWN, (n + 1) * OWN)
            yacc[rows, :] += mm(ab, wproj[fs, rows])
            dxacc[rows, :] += mm(db, wfc[rows, fs], 1, 1)
        return carry

    lax.fori_loop(0, FF // FC, feed, 0)

    for sl in (1, 0):
        out = half_get(mid, sl) + half_get(yacc, sl) + pb[...]
        xn[sl * SEG : (sl + 1) * SEG, :] = out.astype(bf16)
    hid_cp = remote(xn.at[pl.ds(SEG, SEG)], hid_h.at[y], out_s.at[0], out_r.at[0], far)
    hid_cp.start()
    hid_lo = pltpu.make_async_copy(xn.at[pl.ds(0, SEG)], hid_h.at[y], loc_out.at[0])
    hid_lo.start()

    def do_copy(sl):
        blk = bl if sl == 0 else br
        dst = xn.at[pl.ds(OWN, OWN), pl.ds(aligned(blk * SEG, SEG), SEG)]
        return remote(oTf.at[sl, pl.ds(0, OWN)], dst, d_s.at[sl], d_r.at[sl], sib)

    for sl in (0, 1):
        blk = bl if sl == 0 else br
        rows = slice(sl * SEG, (sl + 1) * SEG)
        gm = cot2[rows, :].astype(f32) + norm_back(half_get(mid, sl), half_get(dxacc, sl) * mg[...])
        half_put(dxacc, sl, gm)
        gmb = gm.astype(bf16)
        oTf[sl, 0:OWN, :] = mm(wout[pl.ds(ow, OWN), :], gmb, 1, 1).astype(bf16)
        do_copy(sl).start()
        xn[OWN:D, pl.ds(aligned(blk * SEG, SEG), SEG)] = mm(wout[pl.ds(cw, OWN), :], gmb, 1, 1).astype(bf16)

    dk = yacc
    dv = mid
    dk[...] = jnp.zeros_like(dk)
    dv[...] = jnp.zeros_like(dv)
    for cp in (do_copy(0), do_copy(1)):
        cp.wait()
    for b in range(NB):
        cols = slice(b * SEG, (b + 1) * SEG)
        li = linv[:, cols]
        dof = xn[OWN:D, cols].astype(f32)
        prod = dof * oTo[b].astype(f32)
        dl = jnp.concatenate(
            [jnp.sum(prod[h * HD : (h + 1) * HD], axis=0, keepdims=True) for h in range(NH)], axis=0
        ) * li
        deltap[:, cols] = dl
        dos = (dof * rep(li, HD)).astype(bf16)
        spread(wproj, cols, dos.T)
        dpp = mm(pvbd[...], dos)
        dsb = (ep[:, cols].astype(f32) * (dpp - rep(dl, PP))).astype(bf16)
        dsp[:, cols] = dsb
        dqT[:, cols] = mm(pkT[...], dsb)

    def prefix_grad(left, right, at):
        for n in range(2):
            t = mm(left, right[0:1024, n * 512 : (n + 1) * 512])
            for p in range(2):
                h = 4 * n + 2 * p
                v = t[h * PP : (h + 1) * PP, 2 * p * 128 : (2 * p + 1) * 128]
                v = v + t[(h + 1) * PP : (h + 2) * PP, (2 * p + 1) * 128 : (2 * p + 2) * 128]
                gown[at + h // 2] = v

    prefix_grad(dsp[...], qm, 0)
    prefix_grad(ep[...], wproj, NRED // 2)

    def across(src_ref, dst_ref, ss, rsm, j):
        return pltpu.make_async_remote_copy(
            src_ref=src_ref, dst_ref=dst_ref, send_sem=ss, recv_sem=rsm, device_id={"dp": j}, device_id_type=MESH
        )

    def others(n, fn):
        def step(j, carry):
            @pl.when(j != dp)
            def _():
                fn(j)
            return carry

        lax.fori_loop(0, n, step, 0)

    mychunk = c * NRED + dp

    def p1_copy(j):
        return across(gown.at[j], rs.at[dp], p1_s.at[j], p1_r.at[dp], j)

    def p1_back(j):
        return across(gown.at[0], rs.at[j], p1_s.at[0], p1_r.at[j], j)

    def p2_copy(j):
        return across(gfull.at[mychunk], gfull.at[mychunk], p2_s.at[j], p2_r.at[dp], j)

    def p2_back(j):
        return across(gfull.at[0], gfull.at[c * NRED + j], p2_s.at[0], p2_r.at[j], j)

    def pb_copy():
        return remote(red.at[0], red.at[1], pb_s.at[0], pb_r.at[0], far)

    def pc_copy():
        mine = gfull.at[pl.ds(c * NRED, NRED)]
        return remote(mine, mine, pb_s.at[1], pb_r.at[1], sib)

    def prefix_sum(stage):
        if stage == 0:
            others(NRED, lambda j: p1_copy(j).start())

            @pl.when(dp < NRED)
            def _():
                rs[dp] = gown[dp]
        elif stage == 1:
            @pl.when(dp < NRED)
            def _():
                others(ndp, lambda j: p1_back(j).wait_recv())
                red[0] = lax.fori_loop(1, ndp, lambda j, a: a + rs[j], rs[0])
                pb_copy().start()
        elif stage == 2:
            @pl.when(dp < NRED)
            def _():
                pb_copy().wait()
                gfull[mychunk] = red[0] + red[1]
                others(ndp, lambda j: p2_copy(j).start())
        elif stage == 3:
            others(NRED, lambda j: p2_back(j).wait_recv())
            pc_copy().start()
        else:
            pc_copy().wait()
            others(NRED, lambda j: p1_copy(j).wait_send())

            @pl.when(dp < NRED)
            def _():
                others(ndp, lambda j: p2_copy(j).wait_send())

    prefix_sum(0)

    def at_tile(i, j):
        qi = jnp.where(y == 1, j, 3 - i)
        ki = jnp.where(y == 1, i, 3 - j)
        return qi, ki

    def tile(i, j):
        qi, ki = at_tile(i, j)
        qr = pl.ds(aligned(qi * SEG, SEG), SEG)
        kr = pl.ds(aligned(ki * SEG, SEG), SEG)
        off = pl.ds(aligned((lax.div(qi * (qi + 1), 2) + ki) * SEG, SEG), SEG)
        sbuf = (dbias, ot.at[pl.ds(0, SEG)])
        dbuf = [vT.at[pl.ds(0, SEG), pl.ds(n * SEG, SEG)] for n in range(4)]

        def stage_a(h):
            sbuf[h % 2][...] = mm(vx[h // 2, kr, :], wproj[qr, h * 128 : (h + 1) * 128], 1, 1)

        def stage_b(h):
            dbuf[h % 4][...] = (
                es[h, off, :].astype(f32) * (sbuf[h % 2][...] - deltap[h : h + 1, qr])
            ).astype(bf16)

        def stage_c(hp):
            hl = slice(hp * 128, (hp + 1) * 128)
            h = 2 * hp
            w0 = slice(h * 128, (h + 1) * 128)
            w1 = slice((h + 1) * 128, (h + 2) * 128)
            d0, d1 = dbuf[h % 4], dbuf[(h + 1) % 4]
            dk[kr, hl] += mm(d0[...], qm[qr, w0]) + mm(d1[...], qm[qr, w1])
            dv[kr, hl] += mm(es[h, off, :], wproj[qr, w0]) + mm(es[h + 1, off, :], wproj[qr, w1])
            for hh, d in ((h, d0), (h + 1, d1)):
                hrows = slice(hh * HD, (hh + 1) * HD)
                dqT[hrows, qr] += mm(kT[hrows, kr], d[...])

        stage_a(0)
        for hp in range(4):
            stage_a(2 * hp + 1)
            stage_b(2 * hp)
            if hp < 3:
                stage_a(2 * hp + 2)
            stage_b(2 * hp + 1)
            if hp:
                stage_c(hp - 1)
        stage_c(3)

    def block_at(i):
        return jnp.where(y == 1, i, 3 - i)

    def d_copy(b, i):
        sl = slot_of(b)
        return remote(
            wfc.at[pl.ds(aligned(sl * SEG, SEG), SEG), pl.ds(2048, 1536)],
            wfc.at[pl.ds(aligned((2 * sl + c) * SEG, SEG), SEG), pl.ds(0, 1536)],
            g_s.at[lax.div(i, 2)], g_r.at[lax.div(i, 2)], sib,
        )

    def done_block(i):
        b = block_at(i)
        br_ = pl.ds(aligned(b * SEG, SEG), SEG)
        sl = slot_of(b)
        mine = lax.rem(b, 2) == c
        parts = (
            (dqT[:, br_] * HD ** (-0.5)).astype(bf16).T,
            dk[br_, :].astype(bf16),
            dv[br_, :].astype(bf16),
        )
        row = aligned(jnp.where(mine, 2 * sl + c, sl) * SEG, SEG)
        for p in range(3):
            col = aligned(jnp.where(mine, 0, 2048) + p * 512, 512)
            wfc[pl.ds(row, SEG), pl.ds(col, 512)] = parts[p]

        @pl.when(jnp.logical_not(mine))
        def _():
            d_copy(b, i).start()

    def finish(i):
        b = block_at(i)
        sl = slot_of(b)

        @pl.when(lax.rem(b, 2) == c)
        def _():
            d_copy(b, i).wait_recv()
            acc = None
            for p in range(3):
                for hf in range(2):
                    a = wfc[pl.ds(aligned((2 * sl + hf) * SEG, SEG), SEG), p * 512 : (p + 1) * 512]
                    t = mm(a, wqkv[:, p * D + hf * OWN : p * D + (hf + 1) * OWN], 1, 1)
                    acc = t if acc is None else acc + t
            rows = pl.ds(aligned(sl * SEG, SEG), SEG)
            rows2 = pl.ds(aligned(OWN + sl * SEG, SEG), SEG)
            gm = jnp.concatenate([dxacc[rows, :], dxacc[rows2, :]], axis=1)
            res = gm + norm_back(tok2[rows, :].astype(f32), acc * ag[...])

            @pl.when(i < 2)
            def _():
                hid_cp.wait_send()

            @pl.when(i >= 2)
            def _():
                hid_lo.wait()

            xn[rows, :] = res.astype(bf16)

            @pl.when(i < 2)
            def _():
                gt_cp().start()

            @pl.when(i >= 2)
            def _():
                gt_lo().start()

    def gt_cp():
        return remote(xn.at[pl.ds(SEG, SEG)], gtok_h.at[y], out_s.at[1], out_r.at[1], far)

    def gt_lo():
        return pltpu.make_async_copy(xn.at[pl.ds(0, SEG)], gtok_h.at[y], loc_out.at[1])

    cot_cp.wait_send()
    def round_of(i, carry):
        lax.fori_loop(i, 4, lambda j, cc: (tile(i, j), cc)[1], 0)

        @pl.when(i < 4)
        def _():
            done_block(i)

        for k in range(3):
            @pl.when(i == k)
            def _(k=k):
                prefix_sum(k + 1)

        @pl.when(i > 0)
        def _():
            finish(i - 1)
        return carry

    lax.fori_loop(0, 5, round_of, 0)
    prefix_sum(4)

    for i in range(2):
        pltpu.make_async_copy(
            wfc.at[pl.ds(0, SEG), pl.ds(2048, 1536)], wfc.at[pl.ds(0, SEG), pl.ds(2048, 1536)], g_s.at[i]
        ).wait()
    gt_lo().wait()
    gt_cp().wait()
    hid_cp.wait_recv()


def layer(args, ndp):
    vm = pl.BlockSpec(memory_space=pltpu.VMEM)
    hb = pl.BlockSpec(memory_space=pl.ANY)
    sm = pl.BlockSpec(memory_space=pltpu.SMEM)
    (tokens, cotangent, src_len, tgt_len, attn_gain, attn_shift, qkv_weight, qkv_bias, out_weight, out_bias,
     mlp_gain, mlp_shift, fc_weight, fc_bias, proj_weight, proj_bias, embed_rows, mid_weight, mid_bias,
     kv_weight, kv_bias) = args
    V = pltpu.VMEM
    dma = pltpu.SemaphoreType.DMA
    return pl.pallas_call(
        functools.partial(kernel, ndp),
        out_shape=(
            jax.ShapeDtypeStruct(tokens.shape, bf16),
            jax.ShapeDtypeStruct(tokens.shape, bf16),
            jax.ShapeDtypeStruct((2 * NRED, PP, 128), f32),
            jax.ShapeDtypeStruct((PP, 512), f32),
        ),
        in_specs=[hb, hb, sm, sm] + [vm] * 10 + [hb] * 4 + [vm, hb, hb],
        out_specs=(hb, hb, vm, vm),
        scratch_shapes=[
            V((D, 3 * D), bf16), V((D, D), bf16), V((D, FF), bf16), V((FF, D), bf16),
            V((OWN, D), bf16), V((OWN, D), bf16), V((D, D), bf16), V((D, D), bf16),
            V((4, PP + D, 128), bf16), V((OWN, D), bf16), V((4, D, 128), bf16), V((NH * VR, D), bf16),
            V((NH, 10 * SEG, SEG), bf16), V((NH * PP, D), bf16), V((NH * PP, D), bf16),
            V((NH * VR, SEG), f32), V((NB, OWN, SEG), bf16), V((2, D, SEG), bf16),
            V((D, OWN), f32), V((D, OWN), f32), V((D, OWN), f32),
            V((OWN, D), f32), V((PP + D, 128), f32), V((SEG, SEG), f32),
            V((OWN, NH * PP), bf16), V((NH * PP, OWN), bf16), V((NH * VR, NH * PP), bf16),
            V((PP, SEG), f32), V((PP, SEG), f32),
            V((NH, D), f32), V((NH, D), f32),
            V((NRED, PP, 128), f32), V((ndp, PP, 128), f32), V((2, PP, 128), f32),
            V((1, D), f32), V((1, D), f32), V((1, 3 * D), f32), V((1, D), f32), V((1, D), f32), V((1, D), f32),
            V((1, FF), f32), V((1, D), f32), V((1, 2 * D), f32),
            dma((12,)), dma((5,)), dma((5,)), dma((5,)), dma((5,)), dma((2,)), dma((2,)),
            dma((2,)), dma((2,)), dma((2,)), dma((2,)), dma((2,)), dma((2,)), dma((2,)),
            dma((NRED,)), dma((ndp,)), dma((2,)), dma((2,)), dma((ndp,)), dma((NRED,)),
        ],
        compiler_params=pltpu.CompilerParams(
            collective_id=0, has_side_effects=True, vmem_limit_bytes=64 << 20
        ),
    )(tokens, cotangent, src_len, tgt_len, attn_gain, attn_shift, qkv_bias, out_bias, mlp_gain, mlp_shift, fc_bias,
      proj_bias, mid_bias, kv_bias, qkv_weight, out_weight, fc_weight, proj_weight, embed_rows, mid_weight, kv_weight)


def reparam_kernel(
    hid_i, gtok_i, gfull, hidden, emb, midw_h, kvw_h,
    hid_o, gtok_o, gemb, gmidw_o, gmidb, gkvw_o, gkvb,
    midw, kvw, gkvw, gmidw, hid_v, gtok_v, sem,
):
    def go(i, a, b):
        cp = pltpu.make_async_copy(a, b, sem.at[i])
        cp.start()
        return cp

    ld_out = [go(2, hid_i, hid_v), go(3, gtok_i, gtok_v)]
    ld_kv = go(0, kvw_h, kvw)
    ld_mid = go(1, midw_h, midw)
    moves = []
    quarter = NRED // 2
    order = [half * NRED + part * quarter + j for part in (0, 1) for half in (0, 1) for j in range(quarter)]
    grad = jnp.concatenate([gfull[i] for i in order], axis=1)
    hid = hidden[...]
    h0, h1, h2 = split3(hid)
    g0, g1, g2 = split3(grad)
    left = jnp.concatenate([h0, h1, h0, h1, h2, h0], axis=0)
    right = jnp.concatenate([g0, g0, g1, g1, g0, g2], axis=0)
    W = 512
    for n in range(2 * D // W):
        gkvw[:, n * W : (n + 1) * W] = mm(left, right[:, n * W : (n + 1) * W], 0, 0)
        moves.append(go(4 + n, gkvw.at[:, pl.ds(n * W, W)], gkvw_o.at[:, pl.ds(n * W, W)]))
    for cp in ld_out:
        cp.wait()
    moves += [go(9, hid_v, hid_o), go(10, gtok_v, gtok_o)]
    gkvb[...] = jnp.sum(grad, axis=0, keepdims=True).reshape(2 * D)
    ld_kv.wait()
    three = mm(jnp.concatenate([g0, g1, g2], axis=0), kvw[...], 1, 1)
    gp = (three[0:PP] + three[PP : 2 * PP] + three[2 * PP :]) * (1.0 - hid * hid)
    gmidb[...] = jnp.sum(gp, axis=0, keepdims=True).reshape(512)
    p0, p1, p2 = split3(gp)
    p3 = jnp.concatenate([p0, p1, p2], axis=0)
    embp = jnp.concatenate([emb[...], jnp.zeros((PP - PRE, D), bf16)], axis=0)
    emb3 = jnp.concatenate([embp] * 3, axis=0)
    gmidw[...] = mm(emb3, p3, 0, 0)
    moves.append(go(8, gmidw, gmidw_o))
    ld_mid.wait()
    back = mm(p3, midw[...], 1, 1)
    gemb[...] = (back[0:PP] + back[PP : 2 * PP] + back[2 * PP :])[0:PRE]
    for cp in moves:
        cp.wait()


def on_device(ndp, *args):
    embed_rows, mid_weight, _, kv_weight, _ = args[16:]
    hidden_out, grad_tokens, gfull, hidden = layer(args, ndp)
    vm = pl.BlockSpec(memory_space=pltpu.VMEM)
    hb = pl.BlockSpec(memory_space=pl.ANY)
    sds = jax.ShapeDtypeStruct
    return pl.pallas_call(
        reparam_kernel,
        out_shape=(
            sds(hidden_out.shape, bf16), sds(grad_tokens.shape, bf16), sds((PRE, D), f32), sds((D, 512), f32),
            sds((512,), f32), sds((512, 2 * D), f32), sds((2 * D,), f32),
        ),
        in_specs=[hb, hb, vm, vm, vm, hb, hb],
        out_specs=(hb, hb, vm, hb, vm, hb, vm),
        scratch_shapes=[
            pltpu.VMEM((D, 512), bf16), pltpu.VMEM((512, 2 * D), bf16), pltpu.VMEM((512, 2 * D), f32),
            pltpu.VMEM((D, 512), f32), pltpu.VMEM(hidden_out.shape, bf16), pltpu.VMEM(hidden_out.shape, bf16),
            pltpu.SemaphoreType.DMA((11,)),
        ],
        compiler_params=pltpu.CompilerParams(vmem_limit_bytes=64 << 20),
    )(hidden_out, grad_tokens, gfull, hidden, embed_rows, mid_weight, kv_weight)


def solution(mesh):
    split = P("dp", "seq", None)
    return jax.shard_map(
        functools.partial(on_device, mesh.shape["dp"]),
        mesh=mesh,
        in_specs=(split, split, P("dp"), P("dp")) + (P(),) * 17,
        out_specs=(split, split, P(), P(), P(), P(), P()),
        check_vma=False,
    )
```

```python
import functools

import jax
import jax.numpy as jnp
from jax import lax
from jax.experimental import pallas as pl
from jax.experimental.pallas import tpu as pltpu
from jax.sharding import PartitionSpec as P

D = 1024
HD = 64
FF = 4096
PRE = 10
PP = 16
SEG = 256
OWN = 512
NH = 8
NB = 4
NRED = 8
VR = 80
EPS = 1e-05
NEG = -1e30
MESH = pl.DeviceIdType.MESH
f32 = jnp.float32
bf16 = jnp.bfloat16


def mm(a, b, ca=1, cb=0):
    return lax.dot_general(a, b, (((ca,), (cb,)), ((), ())), preferred_element_type=f32)


def centre(v):
    mean = jnp.mean(v, axis=-1, keepdims=True)
    cen = v - mean
    var = jnp.mean(cen * cen, axis=-1, keepdims=True)
    return cen, lax.rsqrt(var + EPS)


def norm_back(v, incoming):
    cen, r = centre(v)
    xhat = cen * r
    m1 = jnp.mean(incoming, axis=-1, keepdims=True)
    m2 = jnp.mean(incoming * xhat, axis=-1, keepdims=True)
    return r * (incoming - m1 - xhat * m2)


def aligned(i, n):
    return pl.multiple_of(i, n)


def split3(v):
    hi = v.astype(bf16)
    rest = v - hi.astype(f32)
    mid = rest.astype(bf16)
    lo = (rest - mid.astype(f32)).astype(bf16)
    return hi, mid, lo


def kernel(
    ndp,
    tok_h, cot_h, src, tgt,
    ag1, ash1, qb1, ob1, mg1, msh1, fb1, pb1, mb1, kvb1,
    wqkv_h, wout_h, wfc_h, wproj_h, emb, midw_h, kvw_h,
    hid_h, gtok_h, gfull, hidden_o,
    wqkv, wout, wfc, wproj,
    tok2, cot2, xn, qm, kx, kT, vx, vT, es, ep, dsp, ot, oTo, oTf,
    mid, yacc, dxacc, dqT, kb, dbias,
    pkT, pvbd, pvT, pc0, pc1, linv, deltap, gown, rs, red,
    ag, ash, qb, ob, mg, msh, fb, pb, kvb,
    wsem, far_s, far_r, xn_s, xn_r, o_s, o_r, d_s, d_r, g_s, g_r, out_s, out_r, loc_out,
    p1_s, p1_r, pb_s, pb_r, p2_s, p2_r,
):
    dp = lax.axis_index("dp")
    s = lax.axis_index("seq")
    y = lax.div(s, 2)
    c = lax.rem(s, 2)
    sib = 2 * y + (1 - c)
    far = 2 * (1 - y) + c
    bl = 2 * y + c
    br = 2 * (1 - y) + c
    cw = aligned(c * OWN, OWN)
    ow = aligned((1 - c) * OWN, OWN)

    def load(i, src_ref, dst_ref):
        cp = pltpu.make_async_copy(src_ref, dst_ref, wsem.at[i])
        cp.start()
        return cp

    ld_tok = load(0, tok_h.at[y], tok2.at[pl.ds(0, SEG)])
    ld_mid0 = load(1, midw_h.at[pl.ds(0, 512)], vT.at[pl.ds(0, 512), pl.ds(0, 512)])
    ld_mid1 = load(2, midw_h.at[pl.ds(512, 512)], vT.at[pl.ds(0, 512), pl.ds(512, 512)])
    ld_kvk = load(3, kvw_h.at[:, pl.ds(cw, OWN)], kT.at[:, pl.ds(0, OWN)])
    ld_kvv = load(4, kvw_h.at[:, pl.ds(aligned(D + c * OWN, OWN), OWN)], kT.at[:, pl.ds(OWN, OWN)])

    barrier = pltpu.get_barrier_semaphore()
    for peer in (sib, far):
        pl.semaphore_signal(barrier, inc=1, device_id={"seq": peer}, device_id_type=MESH)

    def greet(j, carry):
        @pl.when(j != dp)
        def _():
            pl.semaphore_signal(barrier, inc=1, device_id={"dp": j}, device_id_type=MESH)
        return carry

    lax.fori_loop(0, ndp, greet, 0)
    pl.semaphore_wait(barrier, ndp + 1)

    def remote(src_ref, dst_ref, ss, rs, peer):
        return pltpu.make_async_remote_copy(
            src_ref=src_ref, dst_ref=dst_ref, send_sem=ss, recv_sem=rs,
            device_id={"seq": peer}, device_id_type=MESH,
        )

    CH = 64
    NCH = SEG // CH
    tok_cp = [
        remote(
            tok_h.at[1 - y, pl.ds(j * CH, CH)], tok2.at[pl.ds(SEG + j * CH, CH)],
            far_s.at[j], far_r.at[j], far,
        )
        for j in range(NCH)
    ]
    for cp in tok_cp:
        cp.start()
    ld_qkv = load(5, wqkv_h, wqkv)
    cot_cp = remote(cot_h.at[1 - y], cot2.at[pl.ds(SEG, SEG)], far_s.at[NCH], far_r.at[NCH], far)

    for dst, vec in ((ag, ag1), (ash, ash1), (qb, qb1), (ob, ob1), (mg, mg1), (msh, msh1), (fb, fb1), (pb, pb1), (kvb, kvb1)):
        n = vec.shape[0]
        for i in range(0, n, 1024):
            dst[:, i : i + 1024] = vec[pl.ds(i, 1024)].astype(f32).reshape(1, 1024)
    total = src[y] + tgt[y]
    start = src[y]
    rowp = lax.broadcasted_iota(jnp.int32, (PP, 128), 0)
    kb[0:PP, :] = jnp.where(rowp < PRE, 0.0, NEG)
    for b in range(NB):
        pos = lax.broadcasted_iota(jnp.int32, (SEG, 128), 0) + b * SEG
        kb[PP + b * SEG : PP + (b + 1) * SEG, :] = jnp.where(pos < total, 0.0, NEG)

    def norm_rows(row0, n, dst0):
        cen, r = centre(tok2[row0 : row0 + n, :].astype(f32))
        xn[pl.ds(aligned(dst0, n), n), :] = (cen * r * ag[...] + ash[...]).astype(bf16)

    ld_tok.wait()
    norm_rows(0, SEG, bl * SEG)
    xl = xn.at[pl.ds(aligned(bl * SEG, SEG), SEG)]
    xl_cp = remote(xl, xl, xn_s.at[NCH], xn_r.at[NCH], sib)
    xl_cp.start()
    ld_cot = load(6, cot_h.at[y], cot2.at[pl.ds(0, SEG)])
    ld_out = load(7, wout_h, wout)

    ld_mid0.wait()
    ld_mid1.wait()
    embp = jnp.concatenate([emb[...], jnp.zeros((PP - PRE, D), bf16)], axis=0)
    pre = mm(embp[:, 0:512], vT[0:512, 0:512]) + mm(embp[:, 512:1024], vT[0:512, 512:1024])
    pre = pre + mb1[...].astype(f32).reshape(1, 512)
    hidden = jnp.tanh(pre)
    hidden_o[...] = hidden
    ld_kvk.wait()
    ld_kvv.wait()
    h3 = jnp.concatenate(split3(hidden), axis=0)
    pk3 = mm(h3, kT[:, 0:OWN])
    pv3 = mm(h3, kT[:, OWN : 2 * OWN])
    pk = pk3[0:PP] + pk3[PP : 2 * PP] + pk3[2 * PP :] + kvb[:, pl.ds(cw, OWN)]
    pv = pv3[0:PP] + pv3[PP : 2 * PP] + pv3[2 * PP :] + kvb[:, pl.ds(aligned(D + c * OWN, OWN), OWN)]
    for hp in range(4):
        kx[hp, 0:PP, :] = pk[:, hp * 128 : (hp + 1) * 128].astype(bf16)
    hr = lax.broadcasted_iota(jnp.int32, (NH * PP, OWN), 0) // PP
    hc = lax.broadcasted_iota(jnp.int32, (NH * PP, OWN), 1) // HD
    pk8 = jnp.where(hr == hc, jnp.concatenate([pk] * NH, axis=0), 0.0)
    pv8 = jnp.where(hr == hc, jnp.concatenate([pv] * NH, axis=0), 0.0)
    pvbd[...] = pv8.astype(bf16)
    pkT[...] = pk8.T.astype(bf16)
    one_t = jnp.where(lax.broadcasted_iota(jnp.int32, (VR - HD, D), 0) == 0, 1.0, 0.0).astype(bf16)
    pv_t = pv8.T
    up = lax.broadcasted_iota(jnp.int32, (VR - HD, NH * PP), 0)
    for h in range(NH):
        here = lax.broadcasted_iota(jnp.int32, (VR - HD, NH * PP), 1) // PP == h
        vT[h * VR + HD : (h + 1) * VR, :] = one_t
        pvT[h * VR : h * VR + HD, :] = pv_t[h * HD : (h + 1) * HD].astype(bf16)
        pvT[h * VR + HD : (h + 1) * VR, :] = jnp.where(here & (up == 0), 1.0, 0.0).astype(bf16)

    lane = lax.broadcasted_iota(jnp.int32, (1, 128), 1)
    lo_half = jnp.where(lane < HD, 1.0, 0.0).astype(bf16)
    hi_half = jnp.where(lane < HD, 0.0, 1.0).astype(bf16)

    def spread(dst, rows, val):
        for hp in range(4):
            pair = val[:, hp * 128 : (hp + 1) * 128]
            dst[rows, 2 * hp * 128 : (2 * hp + 1) * 128] = pair * lo_half
            dst[rows, (2 * hp + 1) * 128 : (2 * hp + 2) * 128] = pair * hi_half

    def project(b):
        rows = pl.ds(aligned(b * SEG, SEG), SEG)
        krows = pl.ds(aligned(PP + b * SEG, PP), SEG)
        x = xn[rows, :]
        q = (mm(x, wqkv[:, pl.ds(cw, OWN)]) + qb[:, pl.ds(cw, OWN)]).astype(bf16) * jnp.asarray(HD ** (-0.5), bf16)
        spread(qm, rows, q)
        kw = pl.ds(aligned(D + c * OWN, OWN), OWN)
        k = (mm(x, wqkv[:, kw]) + qb[:, kw]).astype(bf16)
        kT[:, rows] = k.T
        vw = pl.ds(aligned(2 * D + c * OWN, OWN), OWN)
        v = (mm(x, wqkv[:, vw]) + qb[:, vw]).astype(bf16)
        vt = v.T
        for h in range(NH):
            vT[h * VR : h * VR + HD, rows] = vt[h * HD : (h + 1) * HD]
        for hp in range(4):
            kx[hp, krows, :] = k[:, hp * 128 : (hp + 1) * 128]
            vx[hp, rows, :] = v[:, hp * 128 : (hp + 1) * 128]

    ld_qkv.wait()
    project(bl)
    xl_cp.wait()
    project(lax.bitwise_xor(bl, 1))

    fw = []
    ld_ffn = []
    for j in range(NCH):
        tok_cp[j].wait_recv()
        if j == NCH - 2:
            cot_cp.start()
        norm_rows(SEG + j * CH, CH, br * SEG + j * CH)
        xr = xn.at[pl.ds(aligned(br * SEG + j * CH, CH), CH)]
        cp = remote(xr, xr, xn_s.at[j], xn_r.at[j], sib)
        cp.start()
        fw.append(cp)
        if j < 2:
            half = pl.ds(j * OWN, OWN)
            ld_ffn.append(load(8 + j, wfc_h.at[half], wfc.at[half]))
        else:
            half = pl.ds((j - 2) * 2 * D, 2 * D)
            ld_ffn.append(load(8 + j, wproj_h.at[half], wproj.at[half]))
    for cp in tok_cp:
        cp.wait_send()
    project(br)
    for cp in fw:
        cp.wait()
    project(lax.bitwise_xor(br, 1))

    def slot_of(b):
        return lax.bitwise_xor(b // 2 if isinstance(b, int) else lax.div(b, 2), y)

    def rep(vals, n):
        return jnp.concatenate([jnp.broadcast_to(vals[h : h + 1], (n, vals.shape[1])) for h in range(NH)], axis=0)

    def twice(v):
        return jnp.concatenate([v, v], axis=1)

    tri = lax.broadcasted_iota(jnp.int32, (SEG, SEG), 0) <= lax.broadcasted_iota(jnp.int32, (SEG, SEG), 1)

    def o_copy(b):
        return remote(
            oTo.at[b], oTf.at[slot_of(b), pl.ds(cw, OWN)], o_s.at[slot_of(b)], o_r.at[slot_of(b)], sib
        )

    scs = ((yacc, pc0), (dxacc, pc1))
    for b in (3, 2, 1, 0):
        cols = slice(b * SEG, (b + 1) * SEG)
        low = PP + b * SEG
        off = SEG * (b * (b + 1) // 2)
        dbias[...] = jnp.where(tri, twice(kb[low : low + SEG, :]), NEG)

        width = (b + 1) * SEG

        def stage_a(h):
            sc, pc = scs[h % 2]
            qh = qm[cols, h * 128 : (h + 1) * 128]
            s0 = mm(kx[h // 2, 0:low, :], qh, 1, 1) + twice(kb[0:low, :])
            pc[...] = s0[0:PP]
            if b:
                sc[0 : b * SEG, 0:SEG] = s0[PP:]
            sc[b * SEG : width, 0:SEG] = mm(kx[h // 2, low : low + SEG, :], qh, 1, 1) + dbias[...]

        def stage_b(h):
            sc, pc = scs[h % 2]
            m = jnp.maximum(
                jnp.max(sc[0:width, 0:SEG], axis=0, keepdims=True), jnp.max(pc[...], axis=0, keepdims=True)
            )
            ep[h * PP : (h + 1) * PP, cols] = jnp.exp(pc[...] - m).astype(bf16)
            es[h, off : off + width, :] = jnp.exp(sc[0:width, 0:SEG] - m).astype(bf16)

        def stage_c(h):
            ot[h * VR : (h + 1) * VR, :] = mm(vT[h * VR : (h + 1) * VR, 0:width], es[h, off : off + width, :])

        stage_a(0)
        for h in range(NH):
            if h + 1 < NH:
                stage_a(h + 1)
            if h:
                stage_c(h - 1)
            stage_b(h)
        stage_c(NH - 1)
        o = ot[...] + mm(pvT[...], ep[:, cols])
        for h in range(NH):
            inv = 1.0 / o[h * VR + HD : h * VR + HD + 1]
            linv[h : h + 1, cols] = inv
            oTo[b, h * HD : (h + 1) * HD, :] = (o[h * VR : h * VR + HD] * inv).astype(bf16)

        @pl.when(c == b % 2)
        def _(b=b):
            oTf[slot_of(b), pl.ds(cw, OWN), :] = oTo[b]

        @pl.when(c != b % 2)
        def _(b=b):
            o_copy(b).start()

    def half_get(ref, sl):
        return jnp.concatenate([ref[sl * SEG : (sl + 1) * SEG, :], ref[OWN + sl * SEG : OWN + (sl + 1) * SEG, :]], axis=1)

    def half_put(ref, sl, val):
        ref[sl * SEG : (sl + 1) * SEG, :] = val[:, 0:OWN]
        ref[OWN + sl * SEG : OWN + (sl + 1) * SEG, :] = val[:, OWN:]

    ld_out.wait()
    ld_cot.wait()
    cot_cp.wait_recv()
    for sl in (0, 1):
        pltpu.make_async_copy(oTf.at[sl, pl.ds(ow, OWN)], oTf.at[sl, pl.ds(ow, OWN)], o_r.at[sl]).wait()
        blk = bl if sl == 0 else br
        m = mm(oTf[sl], wout[...], 0, 0) + ob[...] + tok2[sl * SEG : (sl + 1) * SEG, :].astype(f32)
        half_put(mid, sl, m)
        cen, r = centre(m)
        xn[sl * SEG : (sl + 1) * SEG, :] = (cen * r * mg[...] + msh[...]).astype(bf16)
        pos = lax.broadcasted_iota(jnp.int32, (SEG, 1), 0) + blk * SEG
        seen = jnp.where((pos >= start) & (pos < total), 1.0, 0.0)
        cot2[sl * SEG : (sl + 1) * SEG, :] = (cot2[sl * SEG : (sl + 1) * SEG, :].astype(f32) * seen).astype(bf16)
    for sl in (0, 1):
        pltpu.make_async_copy(oTo.at[sl], oTo.at[sl], o_s.at[sl]).wait()

    for cp in ld_ffn:
        cp.wait()
    yacc[...] = jnp.zeros_like(yacc)
    dxacc[...] = jnp.zeros_like(dxacc)
    FC = 512

    def feed(i, carry):
        fs = pl.ds(aligned(i * FC, FC), FC)
        u = mm(xn[0:OWN, :], wfc[:, fs]) + fb[:, fs]
        da = mm(cot2[...], wproj[fs, :], 1, 1)
        u2 = u * u
        th = jnp.tanh(u * (0.7978845608028654 + 0.035677408136300125 * u2))
        hh = 0.5 * th + 0.5
        act = u * hh
        slope = hh + act * (1.0 - hh) * (1.5957691216057308 + 0.21406444881780075 * u2)
        ab = act.astype(bf16)
        db = (slope * da).astype(bf16)
        for n in range(2):
            rows = slice(n * OWN, (n + 1) * OWN)
            yacc[rows, :] += mm(ab, wproj[fs, rows])
            dxacc[rows, :] += mm(db, wfc[rows, fs], 1, 1)
        return carry

    lax.fori_loop(0, FF // FC, feed, 0)

    for sl in (1, 0):
        out = half_get(mid, sl) + half_get(yacc, sl) + pb[...]
        xn[sl * SEG : (sl + 1) * SEG, :] = out.astype(bf16)
    hid_cp = remote(xn.at[pl.ds(SEG, SEG)], hid_h.at[y], out_s.at[0], out_r.at[0], far)
    hid_cp.start()
    hid_lo = pltpu.make_async_copy(xn.at[pl.ds(0, SEG)], hid_h.at[y], loc_out.at[0])
    hid_lo.start()

    def do_copy(sl):
        blk = bl if sl == 0 else br
        dst = xn.at[pl.ds(OWN, OWN), pl.ds(aligned(blk * SEG, SEG), SEG)]
        return remote(oTf.at[sl, pl.ds(0, OWN)], dst, d_s.at[sl], d_r.at[sl], sib)

    for sl in (0, 1):
        blk = bl if sl == 0 else br
        rows = slice(sl * SEG, (sl + 1) * SEG)
        gm = cot2[rows, :].astype(f32) + norm_back(half_get(mid, sl), half_get(dxacc, sl) * mg[...])
        half_put(dxacc, sl, gm)
        gmb = gm.astype(bf16)
        oTf[sl, 0:OWN, :] = mm(wout[pl.ds(ow, OWN), :], gmb, 1, 1).astype(bf16)
        do_copy(sl).start()
        xn[OWN:D, pl.ds(aligned(blk * SEG, SEG), SEG)] = mm(wout[pl.ds(cw, OWN), :], gmb, 1, 1).astype(bf16)

    dk = yacc
    dv = mid
    dk[...] = jnp.zeros_like(dk)
    dv[...] = jnp.zeros_like(dv)
    for cp in (do_copy(0), do_copy(1)):
        cp.wait()
    for b in range(NB):
        cols = slice(b * SEG, (b + 1) * SEG)
        li = linv[:, cols]
        dof = xn[OWN:D, cols].astype(f32)
        prod = dof * oTo[b].astype(f32)
        dl = jnp.concatenate(
            [jnp.sum(prod[h * HD : (h + 1) * HD], axis=0, keepdims=True) for h in range(NH)], axis=0
        ) * li
        deltap[:, cols] = dl
        dos = (dof * rep(li, HD)).astype(bf16)
        spread(wproj, cols, dos.T)
        dpp = mm(pvbd[...], dos)
        dsb = (ep[:, cols].astype(f32) * (dpp - rep(dl, PP))).astype(bf16)
        dsp[:, cols] = dsb
        dqT[:, cols] = mm(pkT[...], dsb)

    def prefix_grad(left, right, at):
        for n in range(2):
            t = mm(left, right[0:1024, n * 512 : (n + 1) * 512])
            for p in range(2):
                h = 4 * n + 2 * p
                v = t[h * PP : (h + 1) * PP, 2 * p * 128 : (2 * p + 1) * 128]
                v = v + t[(h + 1) * PP : (h + 2) * PP, (2 * p + 1) * 128 : (2 * p + 2) * 128]
                gown[at + h // 2] = v

    prefix_grad(dsp[...], qm, 0)
    prefix_grad(ep[...], wproj, NRED // 2)

    def across(src_ref, dst_ref, ss, rsm, j):
        return pltpu.make_async_remote_copy(
            src_ref=src_ref, dst_ref=dst_ref, send_sem=ss, recv_sem=rsm, device_id={"dp": j}, device_id_type=MESH
        )

    def others(n, fn):
        def step(j, carry):
            @pl.when(j != dp)
            def _():
                fn(j)
            return carry

        lax.fori_loop(0, n, step, 0)

    mychunk = c * NRED + dp

    def p1_copy(j):
        return across(gown.at[j], rs.at[dp], p1_s.at[j], p1_r.at[dp], j)

    def p1_back(j):
        return across(gown.at[0], rs.at[j], p1_s.at[0], p1_r.at[j], j)

    def p2_copy(j):
        return across(gfull.at[mychunk], gfull.at[mychunk], p2_s.at[j], p2_r.at[dp], j)

    def p2_back(j):
        return across(gfull.at[0], gfull.at[c * NRED + j], p2_s.at[0], p2_r.at[j], j)

    def pb_copy():
        return remote(red.at[0], red.at[1], pb_s.at[0], pb_r.at[0], far)

    def pc_copy():
        mine = gfull.at[pl.ds(c * NRED, NRED)]
        return remote(mine, mine, pb_s.at[1], pb_r.at[1], sib)

    def prefix_sum(stage):
        if stage == 0:
            others(NRED, lambda j: p1_copy(j).start())

            @pl.when(dp < NRED)
            def _():
                rs[dp] = gown[dp]
        elif stage == 1:
            @pl.when(dp < NRED)
            def _():
                others(ndp, lambda j: p1_back(j).wait_recv())
                red[0] = lax.fori_loop(1, ndp, lambda j, a: a + rs[j], rs[0])
                pb_copy().start()
        elif stage == 2:
            @pl.when(dp < NRED)
            def _():
                pb_copy().wait()
                gfull[mychunk] = red[0] + red[1]
                others(ndp, lambda j: p2_copy(j).start())
        elif stage == 3:
            others(NRED, lambda j: p2_back(j).wait_recv())
            pc_copy().start()
        else:
            pc_copy().wait()
            others(NRED, lambda j: p1_copy(j).wait_send())

            @pl.when(dp < NRED)
            def _():
                others(ndp, lambda j: p2_copy(j).wait_send())

    prefix_sum(0)

    def at_tile(i, j):
        qi = jnp.where(y == 1, j, 3 - i)
        ki = jnp.where(y == 1, i, 3 - j)
        return qi, ki

    def tile(i, j):
        qi, ki = at_tile(i, j)
        qr = pl.ds(aligned(qi * SEG, SEG), SEG)
        kr = pl.ds(aligned(ki * SEG, SEG), SEG)
        off = pl.ds(aligned((lax.div(qi * (qi + 1), 2) + ki) * SEG, SEG), SEG)
        sbuf = (dbias, ot.at[pl.ds(0, SEG)])
        dbuf = [vT.at[pl.ds(0, SEG), pl.ds(n * SEG, SEG)] for n in range(4)]

        def stage_a(h):
            sbuf[h % 2][...] = mm(vx[h // 2, kr, :], wproj[qr, h * 128 : (h + 1) * 128], 1, 1)

        def stage_b(h):
            dbuf[h % 4][...] = (
                es[h, off, :].astype(f32) * (sbuf[h % 2][...] - deltap[h : h + 1, qr])
            ).astype(bf16)

        def stage_c(hp):
            hl = slice(hp * 128, (hp + 1) * 128)
            h = 2 * hp
            w0 = slice(h * 128, (h + 1) * 128)
            w1 = slice((h + 1) * 128, (h + 2) * 128)
            d0, d1 = dbuf[h % 4], dbuf[(h + 1) % 4]
            dk[kr, hl] += mm(d0[...], qm[qr, w0]) + mm(d1[...], qm[qr, w1])
            dv[kr, hl] += mm(es[h, off, :], wproj[qr, w0]) + mm(es[h + 1, off, :], wproj[qr, w1])
            for hh, d in ((h, d0), (h + 1, d1)):
                hrows = slice(hh * HD, (hh + 1) * HD)
                dqT[hrows, qr] += mm(kT[hrows, kr], d[...])

        stage_a(0)
        for hp in range(4):
            stage_a(2 * hp + 1)
            stage_b(2 * hp)
            if hp < 3:
                stage_a(2 * hp + 2)
            stage_b(2 * hp + 1)
            if hp:
                stage_c(hp - 1)
        stage_c(3)

    def block_at(i):
        return jnp.where(y == 1, i, 3 - i)

    def d_copy(b, i):
        sl = slot_of(b)
        return remote(
            wfc.at[pl.ds(aligned(sl * SEG, SEG), SEG), pl.ds(2048, 1536)],
            wfc.at[pl.ds(aligned((2 * sl + c) * SEG, SEG), SEG), pl.ds(0, 1536)],
            g_s.at[lax.div(i, 2)], g_r.at[lax.div(i, 2)], sib,
        )

    def done_block(i):
        b = block_at(i)
        br_ = pl.ds(aligned(b * SEG, SEG), SEG)
        sl = slot_of(b)
        mine = lax.rem(b, 2) == c
        parts = (
            (dqT[:, br_] * HD ** (-0.5)).astype(bf16).T,
            dk[br_, :].astype(bf16),
            dv[br_, :].astype(bf16),
        )
        row = aligned(jnp.where(mine, 2 * sl + c, sl) * SEG, SEG)
        for p in range(3):
            col = aligned(jnp.where(mine, 0, 2048) + p * 512, 512)
            wfc[pl.ds(row, SEG), pl.ds(col, 512)] = parts[p]

        @pl.when(jnp.logical_not(mine))
        def _():
            d_copy(b, i).start()

    def finish(i):
        b = block_at(i)
        sl = slot_of(b)

        @pl.when(lax.rem(b, 2) == c)
        def _():
            d_copy(b, i).wait_recv()
            acc = None
            for p in range(3):
                for hf in range(2):
                    a = wfc[pl.ds(aligned((2 * sl + hf) * SEG, SEG), SEG), p * 512 : (p + 1) * 512]
                    t = mm(a, wqkv[:, p * D + hf * OWN : p * D + (hf + 1) * OWN], 1, 1)
                    acc = t if acc is None else acc + t
            rows = pl.ds(aligned(sl * SEG, SEG), SEG)
            rows2 = pl.ds(aligned(OWN + sl * SEG, SEG), SEG)
            gm = jnp.concatenate([dxacc[rows, :], dxacc[rows2, :]], axis=1)
            res = gm + norm_back(tok2[rows, :].astype(f32), acc * ag[...])

            @pl.when(i < 2)
            def _():
                hid_cp.wait_send()

            @pl.when(i >= 2)
            def _():
                hid_lo.wait()

            xn[rows, :] = res.astype(bf16)

            @pl.when(i < 2)
            def _():
                gt_cp().start()

            @pl.when(i >= 2)
            def _():
                gt_lo().start()

    def gt_cp():
        return remote(xn.at[pl.ds(SEG, SEG)], gtok_h.at[y], out_s.at[1], out_r.at[1], far)

    def gt_lo():
        return pltpu.make_async_copy(xn.at[pl.ds(0, SEG)], gtok_h.at[y], loc_out.at[1])

    cot_cp.wait_send()
    def round_of(i, carry):
        lax.fori_loop(i, 4, lambda j, cc: (tile(i, j), cc)[1], 0)

        @pl.when(i < 4)
        def _():
            done_block(i)

        for k in range(3):
            @pl.when(i == k)
            def _(k=k):
                prefix_sum(k + 1)

        @pl.when(i > 0)
        def _():
            finish(i - 1)
        return carry

    lax.fori_loop(0, 5, round_of, 0)
    prefix_sum(4)

    for i in range(2):
        pltpu.make_async_copy(
            wfc.at[pl.ds(0, SEG), pl.ds(2048, 1536)], wfc.at[pl.ds(0, SEG), pl.ds(2048, 1536)], g_s.at[i]
        ).wait()
    gt_lo().wait()
    gt_cp().wait()
    hid_cp.wait_recv()


def layer(args, ndp):
    vm = pl.BlockSpec(memory_space=pltpu.VMEM)
    hb = pl.BlockSpec(memory_space=pl.ANY)
    sm = pl.BlockSpec(memory_space=pltpu.SMEM)
    (tokens, cotangent, src_len, tgt_len, attn_gain, attn_shift, qkv_weight, qkv_bias, out_weight, out_bias,
     mlp_gain, mlp_shift, fc_weight, fc_bias, proj_weight, proj_bias, embed_rows, mid_weight, mid_bias,
     kv_weight, kv_bias) = args
    V = pltpu.VMEM
    dma = pltpu.SemaphoreType.DMA
    return pl.pallas_call(
        functools.partial(kernel, ndp),
        out_shape=(
            jax.ShapeDtypeStruct(tokens.shape, bf16),
            jax.ShapeDtypeStruct(tokens.shape, bf16),
            jax.ShapeDtypeStruct((2 * NRED, PP, 128), f32),
            jax.ShapeDtypeStruct((PP, 512), f32),
        ),
        in_specs=[hb, hb, sm, sm] + [vm] * 10 + [hb] * 4 + [vm, hb, hb],
        out_specs=(hb, hb, vm, vm),
        scratch_shapes=[
            V((D, 3 * D), bf16), V((D, D), bf16), V((D, FF), bf16), V((FF, D), bf16),
            V((OWN, D), bf16), V((OWN, D), bf16), V((D, D), bf16), V((D, D), bf16),
            V((4, PP + D, 128), bf16), V((OWN, D), bf16), V((4, D, 128), bf16), V((NH * VR, D), bf16),
            V((NH, 10 * SEG, SEG), bf16), V((NH * PP, D), bf16), V((NH * PP, D), bf16),
            V((NH * VR, SEG), f32), V((NB, OWN, SEG), bf16), V((2, D, SEG), bf16),
            V((D, OWN), f32), V((D, OWN), f32), V((D, OWN), f32),
            V((OWN, D), f32), V((PP + D, 128), f32), V((SEG, SEG), f32),
            V((OWN, NH * PP), bf16), V((NH * PP, OWN), bf16), V((NH * VR, NH * PP), bf16),
            V((PP, SEG), f32), V((PP, SEG), f32),
            V((NH, D), f32), V((NH, D), f32),
            V((NRED, PP, 128), f32), V((ndp, PP, 128), f32), V((2, PP, 128), f32),
            V((1, D), f32), V((1, D), f32), V((1, 3 * D), f32), V((1, D), f32), V((1, D), f32), V((1, D), f32),
            V((1, FF), f32), V((1, D), f32), V((1, 2 * D), f32),
            dma((12,)), dma((5,)), dma((5,)), dma((5,)), dma((5,)), dma((2,)), dma((2,)),
            dma((2,)), dma((2,)), dma((2,)), dma((2,)), dma((2,)), dma((2,)), dma((2,)),
            dma((NRED,)), dma((ndp,)), dma((2,)), dma((2,)), dma((ndp,)), dma((NRED,)),
        ],
        compiler_params=pltpu.CompilerParams(
            collective_id=0, has_side_effects=True, vmem_limit_bytes=64 << 20
        ),
    )(tokens, cotangent, src_len, tgt_len, attn_gain, attn_shift, qkv_bias, out_bias, mlp_gain, mlp_shift, fc_bias,
      proj_bias, mid_bias, kv_bias, qkv_weight, out_weight, fc_weight, proj_weight, embed_rows, mid_weight, kv_weight)


def reparam_kernel(
    hid_i, gtok_i, gfull, hidden, emb, midw_h, kvw_h,
    hid_o, gtok_o, gemb, gmidw_o, gmidb, gkvw_o, gkvb,
    midw, kvw, gkvw, gmidw, hid_v, gtok_v, sem,
):
    def go(i, a, b):
        cp = pltpu.make_async_copy(a, b, sem.at[i])
        cp.start()
        return cp

    ld_out = [go(2, hid_i, hid_v), go(3, gtok_i, gtok_v)]
    ld_kv = go(0, kvw_h, kvw)
    ld_mid = go(1, midw_h, midw)
    moves = []
    quarter = NRED // 2
    order = [half * NRED + part * quarter + j for part in (0, 1) for half in (0, 1) for j in range(quarter)]
    grad = jnp.concatenate([gfull[i] for i in order], axis=1)
    hid = hidden[...]
    h0, h1, h2 = split3(hid)
    g0, g1, g2 = split3(grad)
    left = jnp.concatenate([h0, h1, h0, h1, h2, h0], axis=0)
    right = jnp.concatenate([g0, g0, g1, g1, g0, g2], axis=0)
    W = 512
    for n in range(2 * D // W):
        gkvw[:, n * W : (n + 1) * W] = mm(left, right[:, n * W : (n + 1) * W], 0, 0)
        moves.append(go(4 + n, gkvw.at[:, pl.ds(n * W, W)], gkvw_o.at[:, pl.ds(n * W, W)]))
    for cp in ld_out:
        cp.wait()
    moves += [go(9, hid_v, hid_o), go(10, gtok_v, gtok_o)]
    gkvb[...] = jnp.sum(grad, axis=0, keepdims=True).reshape(2 * D)
    ld_kv.wait()
    three = mm(jnp.concatenate([g0, g1, g2], axis=0), kvw[...], 1, 1)
    gp = (three[0:PP] + three[PP : 2 * PP] + three[2 * PP :]) * (1.0 - hid * hid)
    gmidb[...] = jnp.sum(gp, axis=0, keepdims=True).reshape(512)
    p0, p1, p2 = split3(gp)
    p3 = jnp.concatenate([p0, p1, p2], axis=0)
    embp = jnp.concatenate([emb[...], jnp.zeros((PP - PRE, D), bf16)], axis=0)
    emb3 = jnp.concatenate([embp] * 3, axis=0)
    gmidw[...] = mm(emb3, p3, 0, 0)
    moves.append(go(8, gmidw, gmidw_o))
    ld_mid.wait()
    back = mm(p3, midw[...], 1, 1)
    gemb[...] = (back[0:PP] + back[PP : 2 * PP] + back[2 * PP :])[0:PRE]
    for cp in moves:
        cp.wait()


def on_device(ndp, *args):
    embed_rows, mid_weight, _, kv_weight, _ = args[16:]
    hidden_out, grad_tokens, gfull, hidden = layer(args, ndp)
    vm = pl.BlockSpec(memory_space=pltpu.VMEM)
    hb = pl.BlockSpec(memory_space=pl.ANY)
    sds = jax.ShapeDtypeStruct
    return pl.pallas_call(
        reparam_kernel,
        out_shape=(
            sds(hidden_out.shape, bf16), sds(grad_tokens.shape, bf16), sds((PRE, D), f32), sds((D, 512), f32),
            sds((512,), f32), sds((512, 2 * D), f32), sds((2 * D,), f32),
        ),
        in_specs=[hb, hb, vm, vm, vm, hb, hb],
        out_specs=(hb, hb, vm, hb, vm, hb, vm),
        scratch_shapes=[
            pltpu.VMEM((D, 512), bf16), pltpu.VMEM((512, 2 * D), bf16), pltpu.VMEM((512, 2 * D), f32),
            pltpu.VMEM((D, 512), f32), pltpu.VMEM(hidden_out.shape, bf16), pltpu.VMEM(hidden_out.shape, bf16),
            pltpu.SemaphoreType.DMA((11,)),
        ],
        compiler_params=pltpu.CompilerParams(vmem_limit_bytes=64 << 20),
    )(hidden_out, grad_tokens, gfull, hidden, embed_rows, mid_weight, kv_weight)


def solution(mesh):
    split = P("dp", "seq", None)
    return jax.shard_map(
        functools.partial(on_device, mesh.shape["dp"]),
        mesh=mesh,
        in_specs=(split, split, P("dp"), P("dp")) + (P(),) * 17,
        out_specs=(split, split, P(), P(), P(), P(), P()),
        check_vma=False,
    )
```
